32 devices in a mesh: seq: 8 (over z, y), dp: 4 (over x, core).
Axes of the slice: x: 2, y: 2, z: 4, core: 2. Of those that a mesh axis runs over, the one named last changes fastest.
Arguments:
- inputs: float32 [4, 4096, 128], P('dp', 'seq'), may hold values from -6 to 6
- gate_values: float32 [4, 4096, 128], P('dp', 'seq'), may hold values from -6 to 6
- out_grad: float32 [4, 4096, 128], P('dp', 'seq'), may hold values from -6 to 6
- filter_taps: float32 [4096, 128], P('seq'), may hold values from -0.09375 to 0.09375
- skip_gain: float32 [128], replicated, may hold values from -4 to 4
Outputs:
- input_grad: float32 [4, 4096, 128], P('dp', 'seq')
- gate_grad: float32 [4, 4096, 128], P('dp', 'seq')
- filter_grad: float32 [4096, 128], P('seq', 'dp')
The draws below stay inside these ranges and needn't reach their ends.
All inputs are finite; a program needn't handle non-finite values.
Results may differ from the reference program's by a relative error of at most 0.0001.
Values sent between devices are 32-bit elements; how exact they have to be, the bound alone decides.
A program may use at most 64 MiB of HBM per device.

```python
import math
import jax
import jax.numpy as jnp
from jax import lax

CH = 128
LENGTH = 4096
BATCH = 4


def block_levels(own_key, shape, shards, low, top_value):
    loudness = 1.0
    for dim, shards_of in shards:
        draws = jax.random.uniform(jax.random.fold_in(jax.random.fold_in(own_key, 6), dim), (shards_of,), jnp.float32, low / len(shards), top_value / len(shards))
        loudness = loudness * jnp.repeat(jnp.exp(draws), shape[dim] // shards_of).reshape((-1,) + (1,) * (len(shape) - 1 - dim))
    return loudness


def centred(stream_key, dims, width, bound, cuts=(), held_as=jnp.bfloat16):
    array = width * jax.random.normal(stream_key, dims, jnp.float32)
    if cuts:
        array = array * block_levels(stream_key, dims, cuts, -0.22, 0.18)
    return jnp.clip(array, -bound, bound).astype(held_as)


def setup_inputs(seed: int = 0) -> dict:
    key_list = jax.random.split(jax.random.key(seed), 6)
    inputs = centred(key_list[0], (BATCH, LENGTH, CH), 1.0, 6.0, ((0, 4), (1, 8)), jnp.float32)
    gate_values = centred(key_list[1], (BATCH, LENGTH, CH), 1.0, 6.0, ((0, 4), (1, 8)), jnp.float32)
    out_grad = centred(key_list[2], (BATCH, LENGTH, CH), 1.0, 6.0, ((0, 4), (1, 8)), jnp.float32)
    filter_taps = centred(key_list[3], (LENGTH, CH), LENGTH ** -0.5, 0.09375, ((0, 8),), jnp.float32)
    skip_gain = centred(key_list[4], (CH,), 1.0, 4.0, (), jnp.float32)
    return dict(inputs=inputs, gate_values=gate_values, out_grad=out_grad, filter_taps=filter_taps, skip_gain=skip_gain)


def reference(inputs, gate_values, out_grad, filter_taps, skip_gain):
    total = 2 * LENGTH
    filter_spec = jnp.fft.rfft(filter_taps, n=total, axis=0)

    def one_sequence(operands):
        seq_input, seq_gate, seq_grad = operands
        conv_grad = seq_grad * seq_gate
        input_spec = jnp.fft.rfft(seq_input, n=total, axis=0)
        grad_spec = jnp.fft.rfft(conv_grad, n=total, axis=0)
        conv_time = jnp.fft.irfft(filter_spec * input_spec, n=total, axis=0)[:LENGTH].astype(jnp.float32)
        gate_part = seq_grad * (conv_time + skip_gain[None, :] * seq_input)
        corr_time = jnp.fft.irfft(jnp.conj(filter_spec) * grad_spec, n=total, axis=0)[:LENGTH].astype(jnp.float32)
        input_part = corr_time + skip_gain[None, :] * conv_grad
        filter_part = jnp.fft.irfft(jnp.conj(input_spec) * grad_spec, n=total, axis=0)[:LENGTH].astype(jnp.float32)
        return (input_part, gate_part, filter_part)
    input_grad, gate_grad, filter_parts = lax.map(one_sequence, (inputs, gate_values, out_grad))
    filter_grad = lax.optimization_barrier(jnp.sum(filter_parts, axis=0)) / math.sqrt(BATCH * LENGTH)
    return (input_grad, gate_grad, filter_grad)
```

```python
import functools
import math

import jax
import jax.numpy as jnp
import ml_dtypes
import numpy as np
from jax import lax
from jax.experimental import pallas as pl
from jax.experimental.pallas import tpu as pltpu
from jax.sharding import PartitionSpec as P

first_radix = 32


def rotation(product, modulus, direction):
    fraction = (product % modulus).astype(jnp.float32) / modulus
    turned = 2.0 * math.pi * fraction
    return (jnp.cos(turned), direction * jnp.sin(turned))


def contract(formula, matrix, operand):
    return jnp.einsum(
        formula,
        matrix,
        operand,
        precision=lax.Precision.HIGHEST,
        preferred_element_type=jnp.float32,
    )


def complex_apply(formula, table_re, table_im, values_re, values_im):
    result_re = contract(formula, table_re, values_re) - contract(formula, table_im, values_im)
    result_im = contract(formula, table_re, values_im) + contract(formula, table_im, values_re)
    return (result_re, result_im)


def local_forward(values_re, values_im):
    pairs, rows, width = values_re.shape
    second = rows // first_radix
    values_re = values_re.reshape(pairs, first_radix, second, width)
    values_im = values_im.reshape(pairs, first_radix, second, width)
    outer = jnp.arange(first_radix, dtype=jnp.int32)
    inner = jnp.arange(second, dtype=jnp.int32)
    table_re, table_im = rotation(outer[:, None] * outer[None, :], first_radix, -1.0)
    section_re, section_im = complex_apply(
        "ca,mabx->mcbx", table_re, table_im, values_re, values_im
    )
    twist_re, twist_im = rotation(outer[:, None] * inner[None, :], rows, -1.0)
    twist_re = twist_re[None, :, :, None]
    twist_im = twist_im[None, :, :, None]
    turned_re = section_re * twist_re - section_im * twist_im
    turned_im = section_re * twist_im + section_im * twist_re
    table_re, table_im = rotation(inner[:, None] * inner[None, :], second, -1.0)
    return complex_apply("db,mcbx->mcdx", table_re, table_im, turned_re, turned_im)


def local_inverse(spec_re, spec_im):
    pairs, first, second, width = spec_re.shape
    rows = first * second
    outer = jnp.arange(first, dtype=jnp.int32)
    inner = jnp.arange(second, dtype=jnp.int32)
    table_re, table_im = rotation(inner[:, None] * inner[None, :], second, 1.0)
    section_re, section_im = complex_apply("bd,mcdx->mcbx", table_re, table_im, spec_re, spec_im)
    twist_re, twist_im = rotation(outer[:, None] * inner[None, :], rows, 1.0)
    twist_re = twist_re[None, :, :, None]
    twist_im = twist_im[None, :, :, None]
    turned_re = section_re * twist_re - section_im * twist_im
    turned_im = section_re * twist_im + section_im * twist_re
    table_re, table_im = rotation(outer[:, None] * outer[None, :], first, 1.0)
    result_re, result_im = complex_apply("ac,mcbx->mabx", table_re, table_im, turned_re, turned_im)
    return (result_re.reshape(pairs, rows, width), result_im.reshape(pairs, rows, width))


def frequency_labels():
    steps = lax.axis_size("seq")
    own = lax.axis_index("seq")
    local_labels = 2 * own + jnp.arange(2, dtype=jnp.int32)
    all_labels = jnp.arange(2 * steps, dtype=jnp.int32)
    return (local_labels, all_labels)


def forward_spectrum(signal):
    rows, width = signal.shape
    steps = lax.axis_size("seq")
    piece = rows // steps
    double = 2 * steps
    total = double * rows
    columns = lax.all_to_all(
        signal.reshape(1, rows, width), "seq", split_axis=1, concat_axis=0, tiled=True
    )
    block_index = jnp.arange(steps, dtype=jnp.int32)
    freq_index = jnp.arange(double, dtype=jnp.int32)
    table_re, table_im = rotation(freq_index[:, None] * block_index[None, :], double, -1.0)
    coarse_re = contract("kq,qrc->krc", table_re, columns)
    coarse_im = contract("kq,qrc->krc", table_im, columns)
    offsets = lax.axis_index("seq") * piece + jnp.arange(piece, dtype=jnp.int32)
    twist_re, twist_im = rotation(freq_index[:, None] * offsets[None, :], total, -1.0)
    twist_re = twist_re[:, :, None]
    twist_im = twist_im[:, :, None]
    turned_re = coarse_re * twist_re - coarse_im * twist_im
    turned_im = coarse_re * twist_im + coarse_im * twist_re
    moved = lax.all_to_all(
        jnp.stack([turned_re, turned_im]), "seq", split_axis=1, concat_axis=2, tiled=True
    )
    return local_forward(moved[0], moved[1])


def inverse_time(spec_re, spec_im, local_labels, all_labels):
    pairs, first, second, width = spec_re.shape
    rows = first * second
    steps = lax.axis_size("seq")
    double = 2 * steps
    total = double * rows
    time_re, time_im = local_inverse(spec_re, spec_im)
    positions = jnp.arange(rows, dtype=jnp.int32)
    twist_re, twist_im = rotation(local_labels[:, None] * positions[None, :], total, 1.0)
    twist_re = twist_re[:, :, None]
    twist_im = twist_im[:, :, None]
    turned_re = time_re * twist_re - time_im * twist_im
    turned_im = time_re * twist_im + time_im * twist_re
    moved = lax.all_to_all(
        jnp.stack([turned_re, turned_im]), "seq", split_axis=2, concat_axis=1, tiled=True
    )
    block_index = jnp.arange(steps, dtype=jnp.int32)
    table_re, table_im = rotation(block_index[:, None] * all_labels[None, :], double, 1.0)
    result_re = (
        contract("qk,krc->qrc", table_re, moved[0]) - contract("qk,krc->qrc", table_im, moved[1])
    ) / total
    result_im = (
        contract("qk,krc->qrc", table_re, moved[1]) + contract("qk,krc->qrc", table_im, moved[0])
    ) / total
    return (result_re, result_im)


def local(inputs, gate_values, out_grad, filter_taps, skip_gain):
    seq_input = inputs[0]
    seq_gate = gate_values[0]
    seq_grad = out_grad[0]
    rows, width = seq_input.shape
    replicas = lax.axis_size("dp")
    conv_grad = seq_grad * seq_gate
    spec_re, spec_im = forward_spectrum(
        jnp.concatenate([seq_input, conv_grad, filter_taps], axis=1)
    )
    filter_re = spec_re[..., 2 * width :]
    filter_im = spec_im[..., 2 * width :]
    input_re = spec_re[..., :width]
    input_im = spec_im[..., :width]
    grad_re = spec_re[..., width : 2 * width]
    grad_im = spec_im[..., width : 2 * width]
    conv_re = filter_re * input_re - filter_im * input_im
    conv_im = filter_re * input_im + filter_im * input_re
    corr_re = filter_re * grad_re + filter_im * grad_im
    corr_im = filter_re * grad_im - filter_im * grad_re
    taps_re = input_re * grad_re + input_im * grad_im
    taps_im = input_re * grad_im - input_im * grad_re
    packed_re = conv_re - corr_im
    packed_im = conv_im + corr_re
    local_labels, all_labels = frequency_labels()
    result_re, result_im = inverse_time(
        jnp.concatenate([packed_re, taps_re], axis=3),
        jnp.concatenate([packed_im, taps_im], axis=3),
        local_labels,
        all_labels,
    )
    results = jnp.concatenate([result_re, result_im[..., :width]], axis=2)
    timeline = lax.all_to_all(results, "seq", split_axis=0, concat_axis=1, tiled=True)[0]
    conv_time = timeline[:, :width]
    corr_time = timeline[:, timeline.shape[1] - width :]
    taps_time = timeline[:, width : timeline.shape[1] - width]
    taps_time = lax.psum_scatter(taps_time, "dp", scatter_dimension=1, tiled=True)
    gate_part = seq_grad * (conv_time + skip_gain[None, :] * seq_input)
    input_part = corr_time + skip_gain[None, :] * conv_grad
    length_total = rows * lax.axis_size("seq")
    batch_total = replicas * inputs.shape[0]
    filter_part = taps_time / math.sqrt(batch_total * length_total)
    return (input_part[None], gate_part[None], filter_part)


MESH = pl.DeviceIdType.MESH


def split_halves(table):
    high = table.astype(ml_dtypes.bfloat16)
    low = (table - high.astype(np.float64)).astype(ml_dtypes.bfloat16)
    return high, low


def block_tables(rows):
    double = 2 * rows
    place = np.arange(rows)
    turned = 2.0 * np.pi * ((place[:, None] * place[None, :]) % double) / double
    real = np.cos(turned)
    imag = -np.sin(turned)
    imag[:, 0] = 1.0 - 2.0 * (place % 2)
    forward = np.concatenate([real, imag], axis=1)
    weight = np.full((double, 1), 2.0 / double)
    weight[0] = weight[rows] = 1.0 / double
    inverse = forward.T * weight
    return split_halves(forward) + split_halves(inverse)


def dot3(values, high, low):
    top = values.astype(jnp.bfloat16)
    rest = (values - top.astype(jnp.float32)).astype(jnp.bfloat16)
    dot = functools.partial(jnp.dot, preferred_element_type=jnp.float32)
    return dot(top, high) + (dot(rest, high) + dot(top, low))


def kernel(
    steps, replicas, batch_total,
    in_ref, gate_ref, og_ref, taps_ref, skip_ref, fh_any, fl_any, ih_any, il_any,
    ig_ref, gg_ref, fg_ref,
    fh, fl, ih, il, send, recv, tsend, trecv, tall, spec, tspec, prod, tprod, back_send, back_recv, tback_send, tback_recv,
    table_sem, send_sem, recv_sem, tsend_sem, trecv_sem, bsend_sem, brecv_sem, tbsend_sem, tbrecv_sem,
):
    devices = steps * replicas
    own_s = lax.axis_index("seq")
    own_d = lax.axis_index("dp")
    me = own_s * replicas + own_d
    group = own_d * steps + own_s
    rows, width = in_ref.shape
    lanes = 128
    half = 4

    barrier = pltpu.get_barrier_semaphore()

    def greet(i, carry):
        p = lax.rem(me + i, devices)
        pl.semaphore_signal(
            barrier, inc=1, device_id=(p // replicas, lax.rem(p, replicas)), device_id_type=MESH
        )
        return carry

    lax.fori_loop(1, devices, greet, 0)
    tables = [
        pltpu.make_async_copy(src, dst, table_sem.at[k])
        for k, (src, dst) in enumerate([(fh_any, fh), (fl_any, fl), (ih_any, ih), (il_any, il)])
    ]
    for copy in tables:
        copy.start()

    tiles = width // 8
    tall[...] = taps_ref[...].T.reshape(replicas, steps * half, rows)
    mine = tall[own_d]
    for k in range(steps):
        tsend[k] = mine[half * k : half * k + half]
    in_t = in_ref[...].T.reshape(tiles, 8, rows)
    cg_t = (og_ref[...] * gate_ref[...]).T.reshape(tiles, 8, rows)
    top_rows = lax.broadcasted_iota(jnp.int32, (tiles, 8, rows), 1) < half
    send[:, 0] = jnp.where(top_rows, in_t, pltpu.roll(cg_t, half, 1))
    send[:, 1] = jnp.where(top_rows, pltpu.roll(in_t, half, 1), cg_t)
    pl.semaphore_wait(barrier, devices - 1)

    def taps_copy(s):
        return pltpu.make_async_remote_copy(
            src_ref=tsend.at[s], dst_ref=trecv.at[own_s], send_sem=tsend_sem.at[s],
            recv_sem=trecv_sem.at[own_s], device_id=(s, own_d), device_id_type=MESH,
        )

    def taps_arrival(s):
        return pltpu.make_async_remote_copy(
            src_ref=tsend.at[s], dst_ref=trecv.at[s], send_sem=tsend_sem.at[s],
            recv_sem=trecv_sem.at[s], device_id=(s, own_d), device_id_type=MESH,
        )

    def main_copy(p, q):
        s, d = p // replicas, lax.rem(p, replicas)
        g = d * steps + s
        return pltpu.make_async_remote_copy(
            src_ref=send.at[g // 2, lax.rem(g, 2)], dst_ref=recv.at[q // replicas, lax.rem(q, replicas)],
            send_sem=send_sem.at[p], recv_sem=recv_sem.at[q], device_id=(s, d), device_id_type=MESH,
        )

    def start_taps(i, carry):
        taps_copy(lax.rem(own_s + i, steps)).start()
        return carry

    def start_main(i, carry):
        main_copy(lax.rem(me + i, devices), me).start()
        return carry

    lax.fori_loop(1, steps, start_taps, 0)
    lax.fori_loop(1, devices, start_main, 0)
    trecv[own_s] = tsend[own_s]
    recv[own_s, own_d] = send[group // 2, lax.rem(group, 2)]
    for copy in tables:
        copy.wait()

    def wait_taps(i, carry):
        copy = taps_arrival(lax.rem(own_s + i, steps))
        copy.wait_recv()
        copy.wait_send()
        return carry

    def wait_main(i, carry):
        p = lax.rem(me + i, devices)
        copy = main_copy(p, p)
        copy.wait_recv()
        copy.wait_send()
        return carry

    lax.fori_loop(1, steps, wait_taps, 0)
    doubled = jnp.concatenate(
        [jnp.concatenate([trecv[k], trecv[k]], axis=0)[None] for k in range(steps)], axis=0
    ).reshape(steps * 8, rows)
    tspec[...] = dot3(doubled, fh[...], fl[...]).reshape(steps, 8, 2 * rows)
    lax.fori_loop(1, devices, wait_main, 0)
    spec[...] = dot3(recv[...].reshape(devices * 8, rows), fh[...], fl[...]).reshape(
        steps, replicas, 8, 2 * rows
    )

    lane = lax.broadcasted_iota(jnp.int32, (8, lanes), 1)
    upper = lax.broadcasted_iota(jnp.int32, (8, lanes), 0) < half
    sign = (1 - 2 * lax.rem(lane, 2)).astype(jnp.float32)

    def convolve(c, carry):
        re_at = pl.ds(pl.multiple_of(c * lanes, lanes), lanes)
        im_at = pl.ds(pl.multiple_of(rows + c * lanes, lanes), lanes)
        first = (lane + c * lanes) == 0

        def shifted(re, im):
            out_re = [re[0]] + [re[j] + sign * re[j - 1] for j in range(1, steps)]
            out_im = [im[0]] + [im[j] + sign * im[j - 1] for j in range(1, steps)]
            return out_re, out_im

        filt_re, filt_im = shifted(
            [tspec[j, :, re_at] for j in range(steps)], [tspec[j, :, im_at] for j in range(steps)]
        )
        filt_re2 = [jnp.where(first, b, a) for a, b in zip(filt_re, filt_im)]
        filt_im = [jnp.where(first, 0.0, jnp.where(upper, b, -b)) for b in filt_im]
        for d in range(replicas):
            raw_re = [spec[j, d, :, re_at] for j in range(steps)]
            raw_im = [spec[j, d, :, im_at] for j in range(steps)]
            val_re = [jnp.where(upper, raw_re[j], raw_re[steps - 1 - j]) for j in range(steps)]
            val_im = [jnp.where(upper, raw_im[j], raw_im[steps - 1 - j]) for j in range(steps)]
            res_re, res_im = [], []
            for u in range(steps):
                acc_re, acc_im = None, None
                for v in range(u + 1):
                    j = u - v
                    part_re = filt_re[j] * val_re[v] - filt_im[j] * val_im[v]
                    part_im = filt_re2[j] * val_im[v] + filt_im[j] * val_re[v]
                    acc_re = part_re if acc_re is None else acc_re + part_re
                    acc_im = part_im if acc_im is None else acc_im + part_im
                res_re.append(acc_re)
                res_im.append(acc_im)
            for u in range(steps):
                prod[u, d, :, re_at] = jnp.where(upper, res_re[u], res_re[steps - 1 - u])
                prod[u, d, :, im_at] = jnp.where(upper, res_im[u], res_im[steps - 1 - u])
        sums_re, sums_im = [None] * steps, [None] * steps
        for pair in range(replicas // 2):
            a_re = [spec[j, 2 * pair, :, re_at] for j in range(steps)]
            a_im = [spec[j, 2 * pair, :, im_at] for j in range(steps)]
            b_re = [spec[j, 2 * pair + 1, :, re_at] for j in range(steps)]
            b_im = [spec[j, 2 * pair + 1, :, im_at] for j in range(steps)]
            x_re = [jnp.where(upper, a, pltpu.roll(b, half, 0)) for a, b in zip(a_re, b_re)]
            x_im = [jnp.where(upper, a, pltpu.roll(b, half, 0)) for a, b in zip(a_im, b_im)]
            g_re = [jnp.where(upper, pltpu.roll(a, half, 0), b) for a, b in zip(a_re, b_re)]
            g_im = [jnp.where(upper, pltpu.roll(a, half, 0), b) for a, b in zip(a_im, b_im)]
            x_re, x_im = shifted(x_re, x_im)
            x_re2 = [jnp.where(first, b, a) for a, b in zip(x_re, x_im)]
            x_im = [jnp.where(first, 0.0, b) for b in x_im]
            for k in range(steps):
                for t in range(k, steps):
                    j = t - k
                    part_re = g_re[t] * x_re[j] + g_im[t] * x_im[j]
                    part_im = g_im[t] * x_re2[j] - g_re[t] * x_im[j]
                    sums_re[k] = part_re if sums_re[k] is None else sums_re[k] + part_re
                    sums_im[k] = part_im if sums_im[k] is None else sums_im[k] + part_im
        for k in range(steps):
            tprod[k, :, re_at] = sums_re[k] + pltpu.roll(sums_re[k], half, 0)
            tprod[k, :, im_at] = sums_im[k] + pltpu.roll(sums_im[k], half, 0)
        return carry

    lax.fori_loop(0, rows // lanes, convolve, 0)

    back_send[...] = dot3(prod[...].reshape(devices * 8, 2 * rows), ih[...], il[...]).reshape(
        steps, replicas, 8, rows
    )

    def back_copy(p, q):
        s, d = p // replicas, lax.rem(p, replicas)
        g = lax.rem(q, replicas) * steps + q // replicas
        return pltpu.make_async_remote_copy(
            src_ref=back_send.at[s, d], dst_ref=back_recv.at[g // 2, lax.rem(g, 2)],
            send_sem=bsend_sem.at[p], recv_sem=brecv_sem.at[q], device_id=(s, d), device_id_type=MESH,
        )

    def tback_copy(s, q):
        return pltpu.make_async_remote_copy(
            src_ref=tback_send.at[s], dst_ref=tback_recv.at[q], send_sem=tbsend_sem.at[s],
            recv_sem=tbrecv_sem.at[q], device_id=(s, own_d), device_id_type=MESH,
        )

    def start_back(i, carry):
        back_copy(lax.rem(me + i, devices), me).start()
        return carry

    def start_tback(i, carry):
        tback_copy(lax.rem(own_s + i, steps), own_s).start()
        return carry

    lax.fori_loop(1, devices, start_back, 0)
    folded = dot3(tprod[...].reshape(steps * 8, 2 * rows), ih[...], il[...])
    for k in range(steps):
        tback_send[k] = folded[8 * k : 8 * k + half]
    lax.fori_loop(1, steps, start_tback, 0)
    back_recv[group // 2, lax.rem(group, 2)] = back_send[own_s, own_d]
    tback_recv[own_s] = tback_send[own_s]

    def wait_back(i, carry):
        p = lax.rem(me + i, devices)
        copy = back_copy(p, p)
        copy.wait_recv()
        copy.wait_send()
        return carry

    def wait_tback(i, carry):
        s = lax.rem(own_s + i, steps)
        copy = tback_copy(s, s)
        copy.wait_recv()
        copy.wait_send()
        return carry

    lax.fori_loop(1, devices, wait_back, 0)
    even, odd = back_recv[:, 0], back_recv[:, 1]
    conv = jnp.where(top_rows, even, pltpu.roll(odd, half, 1)).reshape(width, rows).T
    corr = jnp.where(top_rows, pltpu.roll(even, half, 1), odd).reshape(width, rows).T
    skip = skip_ref[...]
    gg_ref[...] = og_ref[...] * (conv + skip * in_ref[...])
    ig_ref[...] = corr + skip * (og_ref[...] * gate_ref[...])
    lax.fori_loop(1, steps, wait_tback, 0)
    gathered = jnp.concatenate([tback_recv[k] for k in range(steps)], axis=0)
    fg_ref[...] = gathered.T * (1.0 / math.sqrt(batch_total * rows * steps))


def fused(inputs, gate_values, out_grad, filter_taps, skip_gain, steps, replicas):
    rows, width = filter_taps.shape
    devices = steps * replicas
    double = 2 * rows
    tables = block_tables(rows)
    f32, bf16 = jnp.float32, jnp.bfloat16
    dma = pltpu.SemaphoreType.DMA
    vmem = pl.BlockSpec(memory_space=pltpu.VMEM)
    anywhere = pl.BlockSpec(memory_space=pl.ANY)
    results = pl.pallas_call(
        functools.partial(kernel, steps, replicas, replicas * inputs.shape[0]),
        out_shape=(
            jax.ShapeDtypeStruct((rows, width), f32),
            jax.ShapeDtypeStruct((rows, width), f32),
            jax.ShapeDtypeStruct((rows, width // replicas), f32),
        ),
        in_specs=[vmem] * 5 + [anywhere] * 4,
        out_specs=(vmem, vmem, vmem),
        scratch_shapes=[
            pltpu.VMEM((rows, double), bf16),
            pltpu.VMEM((rows, double), bf16),
            pltpu.VMEM((double, rows), bf16),
            pltpu.VMEM((double, rows), bf16),
            pltpu.VMEM((devices // 2, 2, 8, rows), f32),
            pltpu.VMEM((steps, replicas, 8, rows), f32),
            pltpu.VMEM((steps, 4, rows), f32),
            pltpu.VMEM((steps, 4, rows), f32),
            pltpu.VMEM((replicas, width // replicas, rows), f32),
            pltpu.VMEM((steps, replicas, 8, double), f32),
            pltpu.VMEM((steps, 8, double), f32),
            pltpu.VMEM((steps, replicas, 8, double), f32),
            pltpu.VMEM((steps, 8, double), f32),
            pltpu.VMEM((steps, replicas, 8, rows), f32),
            pltpu.VMEM((devices // 2, 2, 8, rows), f32),
            pltpu.VMEM((steps, 4, rows), f32),
            pltpu.VMEM((steps, 4, rows), f32),
            dma((4,)),
            dma((devices,)),
            dma((devices,)),
            dma((steps,)),
            dma((steps,)),
            dma((devices,)),
            dma((devices,)),
            dma((steps,)),
            dma((steps,)),
        ],
        compiler_params=pltpu.CompilerParams(
            collective_id=0, has_side_effects=True, vmem_limit_bytes=48 * 1024 * 1024
        ),
    )(
        inputs[0], gate_values[0], out_grad[0], filter_taps, skip_gain[None, :],
        *[jnp.asarray(table) for table in tables],
    )
    return results[0][None], results[1][None], results[2]


def solution(mesh):
    placed = (P("dp", "seq", None), P("dp", "seq", None), P("dp", "seq", None), P("seq", None), P())
    steps, replicas = mesh.shape["seq"], mesh.shape["dp"]

    def either(inputs, gate_values, out_grad, filter_taps, skip_gain):
        rows, width = filter_taps.shape
        fits = width == 4 * steps * replicas and replicas % 2 == 0 and rows % 128 == 0 and steps <= 8
        if fits and inputs.shape[0] == 1:
            return fused(inputs, gate_values, out_grad, filter_taps, skip_gain, steps, replicas)
        return local(inputs, gate_values, out_grad, filter_taps, skip_gain)

    return jax.shard_map(
        either,
        mesh=mesh,
        in_specs=placed,
        out_specs=(P("dp", "seq", None), P("dp", "seq", None), P("seq", "dp")),
        check_vma=False,
    )
```

```python
import functools
import math

import jax
import jax.numpy as jnp
import ml_dtypes
import numpy as np
from jax import lax
from jax.experimental import pallas as pl
from jax.experimental.pallas import tpu as pltpu
from jax.sharding import PartitionSpec as P

first_radix = 32


def rotation(product, modulus, direction):
    fraction = (product % modulus).astype(jnp.float32) / modulus
    turned = 2.0 * math.pi * fraction
    return (jnp.cos(turned), direction * jnp.sin(turned))


def contract(formula, matrix, operand):
    return jnp.einsum(
        formula,
        matrix,
        operand,
        precision=lax.Precision.HIGHEST,
        preferred_element_type=jnp.float32,
    )


def complex_apply(formula, table_re, table_im, values_re, values_im):
    result_re = contract(formula, table_re, values_re) - contract(formula, table_im, values_im)
    result_im = contract(formula, table_re, values_im) + contract(formula, table_im, values_re)
    return (result_re, result_im)


def local_forward(values_re, values_im):
    pairs, rows, width = values_re.shape
    second = rows // first_radix
    values_re = values_re.reshape(pairs, first_radix, second, width)
    values_im = values_im.reshape(pairs, first_radix, second, width)
    outer = jnp.arange(first_radix, dtype=jnp.int32)
    inner = jnp.arange(second, dtype=jnp.int32)
    table_re, table_im = rotation(outer[:, None] * outer[None, :], first_radix, -1.0)
    section_re, section_im = complex_apply(
        "ca,mabx->mcbx", table_re, table_im, values_re, values_im
    )
    twist_re, twist_im = rotation(outer[:, None] * inner[None, :], rows, -1.0)
    twist_re = twist_re[None, :, :, None]
    twist_im = twist_im[None, :, :, None]
    turned_re = section_re * twist_re - section_im * twist_im
    turned_im = section_re * twist_im + section_im * twist_re
    table_re, table_im = rotation(inner[:, None] * inner[None, :], second, -1.0)
    return complex_apply("db,mcbx->mcdx", table_re, table_im, turned_re, turned_im)


def local_inverse(spec_re, spec_im):
    pairs, first, second, width = spec_re.shape
    rows = first * second
    outer = jnp.arange(first, dtype=jnp.int32)
    inner = jnp.arange(second, dtype=jnp.int32)
    table_re, table_im = rotation(inner[:, None] * inner[None, :], second, 1.0)
    section_re, section_im = complex_apply("bd,mcdx->mcbx", table_re, table_im, spec_re, spec_im)
    twist_re, twist_im = rotation(outer[:, None] * inner[None, :], rows, 1.0)
    twist_re = twist_re[None, :, :, None]
    twist_im = twist_im[None, :, :, None]
    turned_re = section_re * twist_re - section_im * twist_im
    turned_im = section_re * twist_im + section_im * twist_re
    table_re, table_im = rotation(outer[:, None] * outer[None, :], first, 1.0)
    result_re, result_im = complex_apply("ac,mcbx->mabx", table_re, table_im, turned_re, turned_im)
    return (result_re.reshape(pairs, rows, width), result_im.reshape(pairs, rows, width))


def frequency_labels():
    steps = lax.axis_size("seq")
    own = lax.axis_index("seq")
    local_labels = 2 * own + jnp.arange(2, dtype=jnp.int32)
    all_labels = jnp.arange(2 * steps, dtype=jnp.int32)
    return (local_labels, all_labels)


def forward_spectrum(signal):
    rows, width = signal.shape
    steps = lax.axis_size("seq")
    piece = rows // steps
    double = 2 * steps
    total = double * rows
    columns = lax.all_to_all(
        signal.reshape(1, rows, width), "seq", split_axis=1, concat_axis=0, tiled=True
    )
    block_index = jnp.arange(steps, dtype=jnp.int32)
    freq_index = jnp.arange(double, dtype=jnp.int32)
    table_re, table_im = rotation(freq_index[:, None] * block_index[None, :], double, -1.0)
    coarse_re = contract("kq,qrc->krc", table_re, columns)
    coarse_im = contract("kq,qrc->krc", table_im, columns)
    offsets = lax.axis_index("seq") * piece + jnp.arange(piece, dtype=jnp.int32)
    twist_re, twist_im = rotation(freq_index[:, None] * offsets[None, :], total, -1.0)
    twist_re = twist_re[:, :, None]
    twist_im = twist_im[:, :, None]
    turned_re = coarse_re * twist_re - coarse_im * twist_im
    turned_im = coarse_re * twist_im + coarse_im * twist_re
    moved = lax.all_to_all(
        jnp.stack([turned_re, turned_im]), "seq", split_axis=1, concat_axis=2, tiled=True
    )
    return local_forward(moved[0], moved[1])


def inverse_time(spec_re, spec_im, local_labels, all_labels):
    pairs, first, second, width = spec_re.shape
    rows = first * second
    steps = lax.axis_size("seq")
    double = 2 * steps
    total = double * rows
    time_re, time_im = local_inverse(spec_re, spec_im)
    positions = jnp.arange(rows, dtype=jnp.int32)
    twist_re, twist_im = rotation(local_labels[:, None] * positions[None, :], total, 1.0)
    twist_re = twist_re[:, :, None]
    twist_im = twist_im[:, :, None]
    turned_re = time_re * twist_re - time_im * twist_im
    turned_im = time_re * twist_im + time_im * twist_re
    moved = lax.all_to_all(
        jnp.stack([turned_re, turned_im]), "seq", split_axis=2, concat_axis=1, tiled=True
    )
    block_index = jnp.arange(steps, dtype=jnp.int32)
    table_re, table_im = rotation(block_index[:, None] * all_labels[None, :], double, 1.0)
    result_re = (
        contract("qk,krc->qrc", table_re, moved[0]) - contract("qk,krc->qrc", table_im, moved[1])
    ) / total
    result_im = (
        contract("qk,krc->qrc", table_re, moved[1]) + contract("qk,krc->qrc", table_im, moved[0])
    ) / total
    return (result_re, result_im)


def local(inputs, gate_values, out_grad, filter_taps, skip_gain):
    seq_input = inputs[0]
    seq_gate = gate_values[0]
    seq_grad = out_grad[0]
    rows, width = seq_input.shape
    replicas = lax.axis_size("dp")
    conv_grad = seq_grad * seq_gate
    spec_re, spec_im = forward_spectrum(
        jnp.concatenate([seq_input, conv_grad, filter_taps], axis=1)
    )
    filter_re = spec_re[..., 2 * width :]
    filter_im = spec_im[..., 2 * width :]
    input_re = spec_re[..., :width]
    input_im = spec_im[..., :width]
    grad_re = spec_re[..., width : 2 * width]
    grad_im = spec_im[..., width : 2 * width]
    conv_re = filter_re * input_re - filter_im * input_im
    conv_im = filter_re * input_im + filter_im * input_re
    corr_re = filter_re * grad_re + filter_im * grad_im
    corr_im = filter_re * grad_im - filter_im * grad_re
    taps_re = input_re * grad_re + input_im * grad_im
    taps_im = input_re * grad_im - input_im * grad_re
    packed_re = conv_re - corr_im
    packed_im = conv_im + corr_re
    local_labels, all_labels = frequency_labels()
    result_re, result_im = inverse_time(
        jnp.concatenate([packed_re, taps_re], axis=3),
        jnp.concatenate([packed_im, taps_im], axis=3),
        local_labels,
        all_labels,
    )
    results = jnp.concatenate([result_re, result_im[..., :width]], axis=2)
    timeline = lax.all_to_all(results, "seq", split_axis=0, concat_axis=1, tiled=True)[0]
    conv_time = timeline[:, :width]
    corr_time = timeline[:, timeline.shape[1] - width :]
    taps_time = timeline[:, width : timeline.shape[1] - width]
    taps_time = lax.psum_scatter(taps_time, "dp", scatter_dimension=1, tiled=True)
    gate_part = seq_grad * (conv_time + skip_gain[None, :] * seq_input)
    input_part = corr_time + skip_gain[None, :] * conv_grad
    length_total = rows * lax.axis_size("seq")
    batch_total = replicas * inputs.shape[0]
    filter_part = taps_time / math.sqrt(batch_total * length_total)
    return (input_part[None], gate_part[None], filter_part)


MESH = pl.DeviceIdType.MESH


def split_halves(table):
    high = table.astype(ml_dtypes.bfloat16)
    low = (table - high.astype(np.float64)).astype(ml_dtypes.bfloat16)
    return high, low


def block_tables(rows):
    double = 2 * rows
    place = np.arange(rows)
    turned = 2.0 * np.pi * ((place[:, None] * place[None, :]) % double) / double
    real = np.cos(turned)
    imag = -np.sin(turned)
    imag[:, 0] = 1.0 - 2.0 * (place % 2)
    forward = np.concatenate([real, imag], axis=1)
    weight = np.full((double, 1), 2.0 / double)
    weight[0] = weight[rows] = 1.0 / double
    inverse = forward.T * weight
    return split_halves(forward) + split_halves(inverse)


def dot3(values, high, low):
    top = values.astype(jnp.bfloat16)
    rest = (values - top.astype(jnp.float32)).astype(jnp.bfloat16)
    dot = functools.partial(jnp.dot, preferred_element_type=jnp.float32)
    return dot(top, high) + (dot(rest, high) + dot(top, low))


def kernel(
    steps, replicas, batch_total,
    in_any, gate_any, og_any, taps_any, skip_any, fh_any, fl_any, ih_any, il_any,
    ig_ref, gg_ref, fg_ref,
    inp, gate, og, taps, skip, fh, fl, ih, il,
    tall, tsend, trecv, xsend, xrecv, gsend, grecv,
    rows8, trows8, spec_t, spec_x, spec_g, prod, tprod,
    csend, crecv, rsend, rrecv, bsend, brecv, merged,
    load_sem, tsend_sem, trecv_sem, xsend_sem, xrecv_sem, gsend_sem, grecv_sem,
    csend_sem, crecv_sem, rsend_sem, rrecv_sem, bsend_sem, brecv_sem,
):
    devices = steps * replicas
    pairs = replicas // 2
    own_s = lax.axis_index("seq")
    own_d = lax.axis_index("dp")
    me = own_s * replicas + own_d
    group = own_d * steps + own_s
    rows, width = inp.shape
    lanes = 128
    half = 4

    barrier = pltpu.get_barrier_semaphore()

    def greet(i, carry):
        p = lax.rem(me + i, devices)
        pl.semaphore_signal(
            barrier, inc=1, device_id=(p // replicas, lax.rem(p, replicas)), device_id_type=MESH
        )
        return carry

    loads = [
        pltpu.make_async_copy(src, dst, load_sem.at[k])
        for k, (src, dst) in enumerate([
            (taps_any, taps), (in_any, inp), (og_any, og), (gate_any, gate), (skip_any, skip),
            (fh_any, fh), (fl_any, fl), (ih_any, ih), (il_any, il),
        ])
    ]
    for copy in loads:
        copy.start()
    lax.fori_loop(1, devices, greet, 0)

    def seq_copy(src, dst, src_sem, dst_sem, s, q):
        return pltpu.make_async_remote_copy(
            src_ref=src.at[s], dst_ref=dst.at[q], send_sem=src_sem.at[s],
            recv_sem=dst_sem.at[q], device_id=(s, own_d), device_id_type=MESH,
        )

    def out_copy(src, dst, src_sem, dst_sem, p, q):
        s, d = p // replicas, lax.rem(p, replicas)
        return pltpu.make_async_remote_copy(
            src_ref=src.at[d * steps + s], dst_ref=dst.at[q // replicas, lax.rem(q, replicas)],
            send_sem=src_sem.at[p], recv_sem=dst_sem.at[q], device_id=(s, d), device_id_type=MESH,
        )

    def back_copy(src, dst, src_sem, dst_sem, p, q):
        s, d = p // replicas, lax.rem(p, replicas)
        return pltpu.make_async_remote_copy(
            src_ref=src.at[s, d], dst_ref=dst.at[lax.rem(q, replicas) * steps + q // replicas],
            send_sem=src_sem.at[p], recv_sem=dst_sem.at[q], device_id=(s, d), device_id_type=MESH,
        )

    def over_seq(use):
        def body(i, carry):
            use(lax.rem(own_s + i, steps))
            return carry

        lax.fori_loop(1, steps, body, 0)

    def over_all(use):
        def body(i, carry):
            use(lax.rem(me + stride * i, devices))
            return carry

        lax.fori_loop(1, devices, body, 0)

    t_refs = (tsend, trecv, tsend_sem, trecv_sem)
    x_refs = (xsend, xrecv, xsend_sem, xrecv_sem)
    g_refs = (gsend, grecv, gsend_sem, grecv_sem)
    c_refs = (csend, crecv, csend_sem, crecv_sem)
    r_refs = (rsend, rrecv, rsend_sem, rrecv_sem)
    b_refs = (bsend, brecv, bsend_sem, brecv_sem)

    def to_channels(values, ref):
        turned = values.T
        for k in range(width // half):
            ref[k] = turned[half * k : half * k + half]

    loads[0].wait()
    tall[...] = taps[...].T.reshape(replicas, steps * half, rows)
    mine = tall[own_d]
    for k in range(steps):
        tsend[k] = mine[half * k : half * k + half]
    loads[1].wait()
    to_channels(inp[...], xsend)
    pl.semaphore_wait(barrier, devices - 1)
    over_seq(lambda s: seq_copy(*t_refs, s, own_s).start())
    over_all(lambda p: out_copy(*x_refs, p, me).start())
    loads[2].wait()
    loads[3].wait()
    gate[...] = og[...] * gate[...]
    to_channels(gate[...], gsend)
    over_all(lambda p: out_copy(*g_refs, p, me).start())
    trecv[own_s] = tsend[own_s]
    xrecv[own_s, own_d] = xsend[group]
    grecv[own_s, own_d] = gsend[group]
    for copy in loads[4:]:
        copy.wait()

    lane = lax.broadcasted_iota(jnp.int32, (8, lanes), 1)
    sign = (1 - 2 * lax.rem(lane, 2)).astype(jnp.float32)

    def forward(ref, spec):
        for s in range(steps):
            for d in range(replicas):
                at = half * (d % 2)
                rows8[s * pairs + d // 2, at : at + half] = ref[s, d]
        spec[...] = dot3(rows8[...].reshape(steps * pairs * 8, rows), fh[...], fl[...]).reshape(
            steps, pairs, 8, 2 * rows
        )

    def backward(ref):
        result = dot3(prod[...].reshape(steps * pairs * 8, 2 * rows), ih[...], il[...])
        for s in range(steps):
            for d in range(replicas):
                at = half * (replicas * s + d)
                ref[s, d] = result[at : at + half]

    def slices(c):
        re_at = pl.ds(pl.multiple_of(c * lanes, lanes), lanes)
        im_at = pl.ds(pl.multiple_of(rows + c * lanes, lanes), lanes)
        return re_at, im_at, (lane + c * lanes) == 0

    def shifted(re, im, first):
        out_re = [re[0]] + [re[j] + sign * re[j - 1] for j in range(1, steps)]
        out_im = [im[0]] + [im[j] + sign * im[j - 1] for j in range(1, steps)]
        out_re2 = [jnp.where(first, b, a) for a, b in zip(out_re, out_im)]
        return out_re, [jnp.where(first, 0.0, b) for b in out_im], out_re2

    def add(total, term):
        return term if total is None else total + term

    def filter_blocks(re_at, im_at, first):
        return shifted(
            [spec_t[j, :, re_at] for j in range(steps)], [spec_t[j, :, im_at] for j in range(steps)], first
        )

    def blocks(spec, k, at):
        return [spec[j, k, :, at] for j in range(steps)]

    def convolve(c, carry):
        re_at, im_at, first = slices(c)
        h_re, h_im, h_re2 = filter_blocks(re_at, im_at, first)
        for k in range(pairs):
            x_re, x_im = blocks(spec_x, k, re_at), blocks(spec_x, k, im_at)
            for u in range(steps):
                re, im = None, None
                for v in range(u + 1):
                    j = u - v
                    re = add(re, h_re[j] * x_re[v] - h_im[j] * x_im[v])
                    im = add(im, h_re2[j] * x_im[v] + h_im[j] * x_re[v])
                prod[u, k, :, re_at] = re
                prod[u, k, :, im_at] = im
        return carry

    def correlate(c, carry):
        re_at, im_at, first = slices(c)
        h_re, h_im, h_re2 = filter_blocks(re_at, im_at, first)
        for k in range(pairs):
            g_re, g_im = blocks(spec_g, k, re_at), blocks(spec_g, k, im_at)
            for u in range(steps):
                re, im = None, None
                for v in range(u, steps):
                    j = v - u
                    re = add(re, h_re[j] * g_re[v] + h_im[j] * g_im[v])
                    im = add(im, h_re2[j] * g_im[v] - h_im[j] * g_re[v])
                prod[u, k, :, re_at] = re
                prod[u, k, :, im_at] = im
        return carry

    def correlate_taps(c, carry):
        re_at, im_at, first = slices(c)
        sums_re, sums_im = [None] * steps, [None] * steps
        for k in range(pairs):
            x_re, x_im, x_re2 = shifted(blocks(spec_x, k, re_at), blocks(spec_x, k, im_at), first)
            g_re, g_im = blocks(spec_g, k, re_at), blocks(spec_g, k, im_at)
            for u in range(steps):
                for v in range(u, steps):
                    j = v - u
                    sums_re[u] = add(sums_re[u], g_re[v] * x_re[j] + g_im[v] * x_im[j])
                    sums_im[u] = add(sums_im[u], g_im[v] * x_re2[j] - g_re[v] * x_im[j])
        for u in range(steps):
            tprod[u, :, re_at] = sums_re[u] + pltpu.roll(sums_re[u], half, 0)
            tprod[u, :, im_at] = sums_im[u] + pltpu.roll(sums_im[u], half, 0)
        return carry

    def to_positions(ref):
        for k in range(width // half):
            at = half * (k % 2)
            merged[k // 2, at : at + half] = ref[k]
        return merged[...].reshape(width, rows).T

    over_seq(lambda s: seq_copy(*t_refs, s, s).wait_recv())
    for k in range(steps):
        trows8[k, :half] = trecv[k]
        trows8[k, half:] = trecv[k]
    spec_t[...] = dot3(trows8[...].reshape(steps * 8, rows), fh[...], fl[...]).reshape(steps, 8, 2 * rows)

    over_all(lambda p: out_copy(*x_refs, p, p).wait_recv())
    forward(xrecv, spec_x)
    lax.fori_loop(0, rows // lanes, convolve, 0)
    backward(csend)
    over_all(lambda p: back_copy(*c_refs, p, me).start())

    over_all(lambda p: out_copy(*g_refs, p, p).wait_recv())
    forward(grecv, spec_g)
    lax.fori_loop(0, rows // lanes, correlate, 0)
    backward(rsend)
    over_all(lambda p: back_copy(*r_refs, p, me).start())

    lax.fori_loop(0, rows // lanes, correlate_taps, 0)
    folded = dot3(tprod[...].reshape(steps * 8, 2 * rows), ih[...], il[...])
    for k in range(steps):
        bsend[k] = folded[8 * k : 8 * k + half]
    over_seq(lambda s: seq_copy(*b_refs, s, own_s).start())

    crecv[group] = csend[own_s, own_d]
    rrecv[group] = rsend[own_s, own_d]
    brecv[own_s] = bsend[own_s]

    over_all(lambda p: back_copy(*c_refs, p, p).wait_recv())
    gain = skip[...]
    gg_ref[...] = og[...] * (to_positions(crecv) + gain * inp[...])
    over_all(lambda p: back_copy(*r_refs, p, p).wait_recv())
    ig_ref[...] = to_positions(rrecv) + gain * gate[...]
    over_seq(lambda s: seq_copy(*b_refs, s, s).wait_recv())
    scale = 1.0 / math.sqrt(batch_total * rows * steps)
    fg_ref[...] = scale * jnp.concatenate([brecv[k] for k in range(steps)], axis=0)

    over_seq(lambda s: seq_copy(*t_refs, s, s).wait_send())
    over_seq(lambda s: seq_copy(*b_refs, s, s).wait_send())
    over_all(lambda p: out_copy(*x_refs, p, p).wait_send())
    over_all(lambda p: out_copy(*g_refs, p, p).wait_send())
    over_all(lambda p: back_copy(*c_refs, p, p).wait_send())
    over_all(lambda p: back_copy(*r_refs, p, p).wait_send())


stride = 1


def fused(inputs, gate_values, out_grad, filter_taps, skip_gain, steps, replicas):
    rows, width = filter_taps.shape
    devices = steps * replicas
    pairs = replicas // 2
    double = 2 * rows
    tables = block_tables(rows)
    f32, bf16 = jnp.float32, jnp.bfloat16
    dma = pltpu.SemaphoreType.DMA
    vmem = pl.BlockSpec(memory_space=pltpu.VMEM)
    anywhere = pl.BlockSpec(memory_space=pltpu.HBM)
    block = pltpu.VMEM((rows, width), f32)
    by_seq = pltpu.VMEM((steps, 4, rows), f32)
    by_group = pltpu.VMEM((devices, 4, rows), f32)
    by_device = pltpu.VMEM((steps, replicas, 4, rows), f32)
    spectrum = pltpu.VMEM((steps, pairs, 8, double), f32)
    taps_spectrum = pltpu.VMEM((steps, 8, double), f32)
    input_part, gate_part, filter_part = pl.pallas_call(
        functools.partial(kernel, steps, replicas, replicas * inputs.shape[0]),
        out_shape=(
            jax.ShapeDtypeStruct((rows, width), f32),
            jax.ShapeDtypeStruct((rows, width), f32),
            jax.ShapeDtypeStruct((width // replicas, rows), f32),
        ),
        in_specs=[anywhere] * 9,
        out_specs=(vmem, vmem, vmem),
        scratch_shapes=[block, block, block, block, pltpu.VMEM((1, width), f32)]
        + [pltpu.VMEM((rows, double), bf16)] * 2
        + [pltpu.VMEM((double, rows), bf16)] * 2
        + [pltpu.VMEM((replicas, width // replicas, rows), f32), by_seq, by_seq]
        + [by_group, by_device, by_group, by_device]
        + [pltpu.VMEM((steps * pairs, 8, rows), f32), pltpu.VMEM((steps, 8, rows), f32)]
        + [taps_spectrum, spectrum, spectrum, spectrum, taps_spectrum]
        + [by_device, by_group, by_device, by_group, by_seq, by_seq]
        + [pltpu.VMEM((width // 8, 8, rows), f32), dma((9,))]
        + [dma((n,)) for n in [steps] * 2 + [devices] * 8 + [steps] * 2],
        compiler_params=pltpu.CompilerParams(
            collective_id=0, has_side_effects=True, vmem_limit_bytes=60 * 1024 * 1024
        ),
    )(
        inputs[0], gate_values[0], out_grad[0], filter_taps, skip_gain[None, :],
        *[jnp.asarray(table) for table in tables],
    )
    return input_part[None], gate_part[None], filter_part.T


def solution(mesh):
    placed = (P("dp", "seq", None), P("dp", "seq", None), P("dp", "seq", None), P("seq", None), P())
    steps, replicas = mesh.shape["seq"], mesh.shape["dp"]

    def either(inputs, gate_values, out_grad, filter_taps, skip_gain):
        rows, width = filter_taps.shape
        fits = width == 4 * steps * replicas and replicas % 2 == 0 and rows % 128 == 0 and steps <= 8
        if fits and inputs.shape[0] == 1:
            return fused(inputs, gate_values, out_grad, filter_taps, skip_gain, steps, replicas)
        return local(inputs, gate_values, out_grad, filter_taps, skip_gain)

    return jax.shard_map(
        either,
        mesh=mesh,
        in_specs=placed,
        out_specs=(P("dp", "seq", None), P("dp", "seq", None), P("seq", "dp")),
        check_vma=False,
    )
```

```python
import functools
import math

import jax
import jax.numpy as jnp
import ml_dtypes
import numpy as np
from jax import lax
from jax.experimental import pallas as pl
from jax.experimental.pallas import tpu as pltpu
from jax.sharding import PartitionSpec as P

first_radix = 32


def rotation(product, modulus, direction):
    fraction = (product % modulus).astype(jnp.float32) / modulus
    turned = 2.0 * math.pi * fraction
    return (jnp.cos(turned), direction * jnp.sin(turned))


def contract(formula, matrix, operand):
    return jnp.einsum(
        formula,
        matrix,
        operand,
        precision=lax.Precision.HIGHEST,
        preferred_element_type=jnp.float32,
    )


def complex_apply(formula, table_re, table_im, values_re, values_im):
    result_re = contract(formula, table_re, values_re) - contract(formula, table_im, values_im)
    result_im = contract(formula, table_re, values_im) + contract(formula, table_im, values_re)
    return (result_re, result_im)


def local_forward(values_re, values_im):
    pairs, rows, width = values_re.shape
    second = rows // first_radix
    values_re = values_re.reshape(pairs, first_radix, second, width)
    values_im = values_im.reshape(pairs, first_radix, second, width)
    outer = jnp.arange(first_radix, dtype=jnp.int32)
    inner = jnp.arange(second, dtype=jnp.int32)
    table_re, table_im = rotation(outer[:, None] * outer[None, :], first_radix, -1.0)
    section_re, section_im = complex_apply(
        "ca,mabx->mcbx", table_re, table_im, values_re, values_im
    )
    twist_re, twist_im = rotation(outer[:, None] * inner[None, :], rows, -1.0)
    twist_re = twist_re[None, :, :, None]
    twist_im = twist_im[None, :, :, None]
    turned_re = section_re * twist_re - section_im * twist_im
    turned_im = section_re * twist_im + section_im * twist_re
    table_re, table_im = rotation(inner[:, None] * inner[None, :], second, -1.0)
    return complex_apply("db,mcbx->mcdx", table_re, table_im, turned_re, turned_im)


def local_inverse(spec_re, spec_im):
    pairs, first, second, width = spec_re.shape
    rows = first * second
    outer = jnp.arange(first, dtype=jnp.int32)
    inner = jnp.arange(second, dtype=jnp.int32)
    table_re, table_im = rotation(inner[:, None] * inner[None, :], second, 1.0)
    section_re, section_im = complex_apply("bd,mcdx->mcbx", table_re, table_im, spec_re, spec_im)
    twist_re, twist_im = rotation(outer[:, None] * inner[None, :], rows, 1.0)
    twist_re = twist_re[None, :, :, None]
    twist_im = twist_im[None, :, :, None]
    turned_re = section_re * twist_re - section_im * twist_im
    turned_im = section_re * twist_im + section_im * twist_re
    table_re, table_im = rotation(outer[:, None] * outer[None, :], first, 1.0)
    result_re, result_im = complex_apply("ac,mcbx->mabx", table_re, table_im, turned_re, turned_im)
    return (result_re.reshape(pairs, rows, width), result_im.reshape(pairs, rows, width))


def frequency_labels():
    steps = lax.axis_size("seq")
    own = lax.axis_index("seq")
    local_labels = 2 * own + jnp.arange(2, dtype=jnp.int32)
    all_labels = jnp.arange(2 * steps, dtype=jnp.int32)
    return (local_labels, all_labels)


def forward_spectrum(signal):
    rows, width = signal.shape
    steps = lax.axis_size("seq")
    piece = rows // steps
    double = 2 * steps
    total = double * rows
    columns = lax.all_to_all(
        signal.reshape(1, rows, width), "seq", split_axis=1, concat_axis=0, tiled=True
    )
    block_index = jnp.arange(steps, dtype=jnp.int32)
    freq_index = jnp.arange(double, dtype=jnp.int32)
    table_re, table_im = rotation(freq_index[:, None] * block_index[None, :], double, -1.0)
    coarse_re = contract("kq,qrc->krc", table_re, columns)
    coarse_im = contract("kq,qrc->krc", table_im, columns)
    offsets = lax.axis_index("seq") * piece + jnp.arange(piece, dtype=jnp.int32)
    twist_re, twist_im = rotation(freq_index[:, None] * offsets[None, :], total, -1.0)
    twist_re = twist_re[:, :, None]
    twist_im = twist_im[:, :, None]
    turned_re = coarse_re * twist_re - coarse_im * twist_im
    turned_im = coarse_re * twist_im + coarse_im * twist_re
    moved = lax.all_to_all(
        jnp.stack([turned_re, turned_im]), "seq", split_axis=1, concat_axis=2, tiled=True
    )
    return local_forward(moved[0], moved[1])


def inverse_time(spec_re, spec_im, local_labels, all_labels):
    pairs, first, second, width = spec_re.shape
    rows = first * second
    steps = lax.axis_size("seq")
    double = 2 * steps
    total = double * rows
    time_re, time_im = local_inverse(spec_re, spec_im)
    positions = jnp.arange(rows, dtype=jnp.int32)
    twist_re, twist_im = rotation(local_labels[:, None] * positions[None, :], total, 1.0)
    twist_re = twist_re[:, :, None]
    twist_im = twist_im[:, :, None]
    turned_re = time_re * twist_re - time_im * twist_im
    turned_im = time_re * twist_im + time_im * twist_re
    moved = lax.all_to_all(
        jnp.stack([turned_re, turned_im]), "seq", split_axis=2, concat_axis=1, tiled=True
    )
    block_index = jnp.arange(steps, dtype=jnp.int32)
    table_re, table_im = rotation(block_index[:, None] * all_labels[None, :], double, 1.0)
    result_re = (
        contract("qk,krc->qrc", table_re, moved[0]) - contract("qk,krc->qrc", table_im, moved[1])
    ) / total
    result_im = (
        contract("qk,krc->qrc", table_re, moved[1]) + contract("qk,krc->qrc", table_im, moved[0])
    ) / total
    return (result_re, result_im)


def local(inputs, gate_values, out_grad, filter_taps, skip_gain):
    seq_input = inputs[0]
    seq_gate = gate_values[0]
    seq_grad = out_grad[0]
    rows, width = seq_input.shape
    replicas = lax.axis_size("dp")
    conv_grad = seq_grad * seq_gate
    spec_re, spec_im = forward_spectrum(
        jnp.concatenate([seq_input, conv_grad, filter_taps], axis=1)
    )
    filter_re = spec_re[..., 2 * width :]
    filter_im = spec_im[..., 2 * width :]
    input_re = spec_re[..., :width]
    input_im = spec_im[..., :width]
    grad_re = spec_re[..., width : 2 * width]
    grad_im = spec_im[..., width : 2 * width]
    conv_re = filter_re * input_re - filter_im * input_im
    conv_im = filter_re * input_im + filter_im * input_re
    corr_re = filter_re * grad_re + filter_im * grad_im
    corr_im = filter_re * grad_im - filter_im * grad_re
    taps_re = input_re * grad_re + input_im * grad_im
    taps_im = input_re * grad_im - input_im * grad_re
    packed_re = conv_re - corr_im
    packed_im = conv_im + corr_re
    local_labels, all_labels = frequency_labels()
    result_re, result_im = inverse_time(
        jnp.concatenate([packed_re, taps_re], axis=3),
        jnp.concatenate([packed_im, taps_im], axis=3),
        local_labels,
        all_labels,
    )
    results = jnp.concatenate([result_re, result_im[..., :width]], axis=2)
    timeline = lax.all_to_all(results, "seq", split_axis=0, concat_axis=1, tiled=True)[0]
    conv_time = timeline[:, :width]
    corr_time = timeline[:, timeline.shape[1] - width :]
    taps_time = timeline[:, width : timeline.shape[1] - width]
    taps_time = lax.psum_scatter(taps_time, "dp", scatter_dimension=1, tiled=True)
    gate_part = seq_grad * (conv_time + skip_gain[None, :] * seq_input)
    input_part = corr_time + skip_gain[None, :] * conv_grad
    length_total = rows * lax.axis_size("seq")
    batch_total = replicas * inputs.shape[0]
    filter_part = taps_time / math.sqrt(batch_total * length_total)
    return (input_part[None], gate_part[None], filter_part)


MESH = pl.DeviceIdType.MESH


def split_halves(table):
    high = table.astype(ml_dtypes.bfloat16)
    low = (table - high.astype(np.float64)).astype(ml_dtypes.bfloat16)
    return high, low


def block_tables(rows):
    double = 2 * rows
    place = np.arange(rows)
    turned = 2.0 * np.pi * ((place[:, None] * place[None, :]) % double) / double
    real = np.cos(turned)
    imag = -np.sin(turned)
    imag[:, 0] = 1.0 - 2.0 * (place % 2)
    forward = np.concatenate([real, imag], axis=1)
    weight = np.full((double, 1), 2.0 / double)
    weight[0] = weight[rows] = 1.0 / double
    inverse = forward.T * weight
    return split_halves(forward) + split_halves(inverse)


def dot3(values, high, low):
    top = values.astype(jnp.bfloat16)
    rest = (values - top.astype(jnp.float32)).astype(jnp.bfloat16)
    dot = functools.partial(jnp.dot, preferred_element_type=jnp.float32)
    return dot(top, high) + (dot(rest, high) + dot(top, low))


def kernel(
    steps, replicas, batch_total,
    in_any, gate_any, og_any, taps_any, skip_any, fh_any, fl_any, ih_any, il_any,
    ig_any, gg_any, fg_any,
    inp, gate, og, taps, skip, fh, fl, ih, il,
    tall, tsend, trecv, xsend, xrecv, gsend, grecv,
    rows8, trows8, spec_t, spec_x, spec_g, prod, tprod,
    csend, crecv, rsend, rrecv, bsend, brecv, merged,
    load_sem, tsend_sem, trecv_sem, xsend_sem, xrecv_sem, gsend_sem, grecv_sem,
    csend_sem, crecv_sem, rsend_sem, rrecv_sem, bsend_sem, brecv_sem, store_sem,
):
    devices = steps * replicas
    pairs = replicas // 2
    own_s = lax.axis_index("seq")
    own_d = lax.axis_index("dp")
    me = own_s * replicas + own_d
    group = own_d * steps + own_s
    rows, width = inp.shape
    lanes = 128
    half = 4

    barrier = pltpu.get_barrier_semaphore()

    def greet(i, carry):
        p = lax.rem(me + i, devices)
        pl.semaphore_signal(
            barrier, inc=1, device_id=(p // replicas, lax.rem(p, replicas)), device_id_type=MESH
        )
        return carry

    loads = [
        pltpu.make_async_copy(src, dst, load_sem.at[k])
        for k, (src, dst) in enumerate([
            (taps_any, taps), (in_any, inp), (og_any, og), (gate_any, gate), (skip_any, skip),
            (fh_any, fh), (fl_any, fl), (ih_any, ih), (il_any, il),
        ])
    ]
    for copy in loads:
        copy.start()
    lax.fori_loop(1, devices, greet, 0)

    def seq_copy(src, dst, src_sem, dst_sem, s, q):
        return pltpu.make_async_remote_copy(
            src_ref=src.at[s], dst_ref=dst.at[q], send_sem=src_sem.at[s],
            recv_sem=dst_sem.at[q], device_id=(s, own_d), device_id_type=MESH,
        )

    def out_copy(src, dst, src_sem, dst_sem, p, q):
        s, d = p // replicas, lax.rem(p, replicas)
        return pltpu.make_async_remote_copy(
            src_ref=src.at[d * steps + s], dst_ref=dst.at[q // replicas, lax.rem(q, replicas)],
            send_sem=src_sem.at[p], recv_sem=dst_sem.at[q], device_id=(s, d), device_id_type=MESH,
        )

    def back_copy(src, dst, src_sem, dst_sem, p, q):
        s, d = p // replicas, lax.rem(p, replicas)
        return pltpu.make_async_remote_copy(
            src_ref=src.at[s, d], dst_ref=dst.at[lax.rem(q, replicas) * steps + q // replicas],
            send_sem=src_sem.at[p], recv_sem=dst_sem.at[q], device_id=(s, d), device_id_type=MESH,
        )

    def over_seq(use):
        def body(i, carry):
            use(lax.rem(own_s + i, steps))
            return carry

        lax.fori_loop(1, steps, body, 0)

    def over_all(use):
        def body(i, carry):
            use(lax.rem(me + stride * i, devices))
            return carry

        lax.fori_loop(1, devices, body, 0)

    t_refs = (tsend, trecv, tsend_sem, trecv_sem)
    x_refs = (xsend, xrecv, xsend_sem, xrecv_sem)
    g_refs = (gsend, grecv, gsend_sem, grecv_sem)
    c_refs = (csend, crecv, csend_sem, crecv_sem)
    r_refs = (rsend, rrecv, rsend_sem, rrecv_sem)
    b_refs = (bsend, brecv, bsend_sem, brecv_sem)

    def to_channels(values, ref):
        turned = values.T
        for k in range(width // half):
            ref[k] = turned[half * k : half * k + half]

    loads[0].wait()
    tall[...] = taps[...].T.reshape(replicas, steps * half, rows)
    mine = tall[own_d]
    for k in range(steps):
        tsend[k] = mine[half * k : half * k + half]
    loads[1].wait()
    to_channels(inp[...], xsend)
    pl.semaphore_wait(barrier, devices - 1)
    over_seq(lambda s: seq_copy(*t_refs, s, own_s).start())
    over_all(lambda p: out_copy(*x_refs, p, me).start())
    loads[2].wait()
    loads[3].wait()
    gate[...] = og[...] * gate[...]
    to_channels(gate[...], gsend)
    over_all(lambda p: out_copy(*g_refs, p, me).start())
    trecv[own_s] = tsend[own_s]
    xrecv[own_s, own_d] = xsend[group]
    grecv[own_s, own_d] = gsend[group]
    for copy in loads[4:]:
        copy.wait()

    lane = lax.broadcasted_iota(jnp.int32, (8, lanes), 1)
    sign = (1 - 2 * lax.rem(lane, 2)).astype(jnp.float32)

    def forward(ref, spec):
        for s in range(steps):
            for d in range(replicas):
                at = half * (d % 2)
                rows8[s * pairs + d // 2, at : at + half] = ref[s, d]
        spec[...] = dot3(rows8[...].reshape(steps * pairs * 8, rows), fh[...], fl[...]).reshape(
            steps, pairs, 8, 2 * rows
        )

    def backward(ref):
        result = dot3(prod[...].reshape(steps * pairs * 8, 2 * rows), ih[...], il[...])
        for s in range(steps):
            for d in range(replicas):
                at = half * (replicas * s + d)
                ref[s, d] = result[at : at + half]

    def slices(c):
        re_at = pl.ds(pl.multiple_of(c * lanes, lanes), lanes)
        im_at = pl.ds(pl.multiple_of(rows + c * lanes, lanes), lanes)
        return re_at, im_at, (lane + c * lanes) == 0

    def shifted(re, im, first):
        out_re = [re[0]] + [re[j] + sign * re[j - 1] for j in range(1, steps)]
        out_im = [im[0]] + [im[j] + sign * im[j - 1] for j in range(1, steps)]
        out_re2 = [jnp.where(first, b, a) for a, b in zip(out_re, out_im)]
        return out_re, [jnp.where(first, 0.0, b) for b in out_im], out_re2

    def add(total, term):
        return term if total is None else total + term

    def filter_blocks(re_at, im_at, first):
        return shifted(
            [spec_t[j, :, re_at] for j in range(steps)], [spec_t[j, :, im_at] for j in range(steps)], first
        )

    def blocks(spec, k, at):
        return [spec[j, k, :, at] for j in range(steps)]

    def convolve(c, carry):
        re_at, im_at, first = slices(c)
        h_re, h_im, h_re2 = filter_blocks(re_at, im_at, first)
        for k in range(pairs):
            x_re, x_im = blocks(spec_x, k, re_at), blocks(spec_x, k, im_at)
            for u in range(steps):
                re, im = None, None
                for v in range(u + 1):
                    j = u - v
                    re = add(re, h_re[j] * x_re[v] - h_im[j] * x_im[v])
                    im = add(im, h_re2[j] * x_im[v] + h_im[j] * x_re[v])
                prod[u, k, :, re_at] = re
                prod[u, k, :, im_at] = im
        return carry

    def correlate(c, carry):
        re_at, im_at, first = slices(c)
        h_re, h_im, h_re2 = filter_blocks(re_at, im_at, first)
        for k in range(pairs):
            g_re, g_im = blocks(spec_g, k, re_at), blocks(spec_g, k, im_at)
            for u in range(steps):
                re, im = None, None
                for v in range(u, steps):
                    j = v - u
                    re = add(re, h_re[j] * g_re[v] + h_im[j] * g_im[v])
                    im = add(im, h_re2[j] * g_im[v] - h_im[j] * g_re[v])
                prod[u, k, :, re_at] = re
                prod[u, k, :, im_at] = im
        return carry

    def correlate_taps(c, carry):
        re_at, im_at, first = slices(c)
        sums_re, sums_im = [None] * steps, [None] * steps
        for k in range(pairs):
            x_re, x_im, x_re2 = shifted(blocks(spec_x, k, re_at), blocks(spec_x, k, im_at), first)
            g_re, g_im = blocks(spec_g, k, re_at), blocks(spec_g, k, im_at)
            for u in range(steps):
                for v in range(u, steps):
                    j = v - u
                    sums_re[u] = add(sums_re[u], g_re[v] * x_re[j] + g_im[v] * x_im[j])
                    sums_im[u] = add(sums_im[u], g_im[v] * x_re2[j] - g_re[v] * x_im[j])
        for u in range(steps):
            tprod[u, :, re_at] = sums_re[u] + pltpu.roll(sums_re[u], half, 0)
            tprod[u, :, im_at] = sums_im[u] + pltpu.roll(sums_im[u], half, 0)
        return carry

    def to_positions(ref):
        for k in range(width // half):
            at = half * (k % 2)
            merged[k // 2, at : at + half] = ref[k]
        return merged[...].reshape(width, rows).T

    over_seq(lambda s: seq_copy(*t_refs, s, s).wait_recv())
    for k in range(steps):
        trows8[k, :half] = trecv[k]
        trows8[k, half:] = trecv[k]
    spec_t[...] = dot3(trows8[...].reshape(steps * 8, rows), fh[...], fl[...]).reshape(steps, 8, 2 * rows)

    over_all(lambda p: out_copy(*x_refs, p, p).wait_recv())
    forward(xrecv, spec_x)
    lax.fori_loop(0, rows // lanes, convolve, 0)
    backward(csend)
    over_all(lambda p: back_copy(*c_refs, p, me).start())

    over_all(lambda p: out_copy(*g_refs, p, p).wait_recv())
    forward(grecv, spec_g)
    lax.fori_loop(0, rows // lanes, correlate, 0)
    backward(rsend)
    over_all(lambda p: back_copy(*r_refs, p, me).start())

    lax.fori_loop(0, rows // lanes, correlate_taps, 0)
    folded = dot3(tprod[...].reshape(steps * 8, 2 * rows), ih[...], il[...])
    for k in range(steps):
        bsend[k] = folded[8 * k : 8 * k + half]
    over_seq(lambda s: seq_copy(*b_refs, s, own_s).start())

    crecv[group] = csend[own_s, own_d]
    rrecv[group] = rsend[own_s, own_d]
    brecv[own_s] = bsend[own_s]

    over_all(lambda p: back_copy(*c_refs, p, p).wait_recv())
    gain = skip[...]
    og[...] = og[...] * (to_positions(crecv) + gain * inp[...])
    stores = [
        pltpu.make_async_copy(src, dst, store_sem.at[k])
        for k, (src, dst) in enumerate([(og, gg_any), (gate, ig_any), (tall.at[0], fg_any)])
    ]
    stores[0].start()
    over_all(lambda p: back_copy(*r_refs, p, p).wait_recv())
    gate[...] = to_positions(rrecv) + gain * gate[...]
    stores[1].start()
    over_seq(lambda s: seq_copy(*b_refs, s, s).wait_recv())
    scale = 1.0 / math.sqrt(batch_total * rows * steps)
    tall[0] = scale * jnp.concatenate([brecv[k] for k in range(steps)], axis=0)
    stores[2].start()

    over_seq(lambda s: seq_copy(*t_refs, s, s).wait_send())
    over_seq(lambda s: seq_copy(*b_refs, s, s).wait_send())
    over_all(lambda p: out_copy(*x_refs, p, p).wait_send())
    over_all(lambda p: out_copy(*g_refs, p, p).wait_send())
    over_all(lambda p: back_copy(*c_refs, p, p).wait_send())
    over_all(lambda p: back_copy(*r_refs, p, p).wait_send())
    for copy in stores:
        copy.wait()


def hand_over(*refs):
    moves = [pltpu.make_async_copy(refs[k], refs[3 + k], refs[6].at[k]) for k in range(3)]
    for copy in moves:
        copy.start()
    for copy in moves:
        copy.wait()


stride = 1


def fused(inputs, gate_values, out_grad, filter_taps, skip_gain, steps, replicas):
    rows, width = filter_taps.shape
    devices = steps * replicas
    pairs = replicas // 2
    double = 2 * rows
    tables = block_tables(rows)
    f32, bf16 = jnp.float32, jnp.bfloat16
    dma = pltpu.SemaphoreType.DMA
    anywhere = pl.BlockSpec(memory_space=pltpu.HBM)
    block = pltpu.VMEM((rows, width), f32)
    by_seq = pltpu.VMEM((steps, 4, rows), f32)
    by_group = pltpu.VMEM((devices, 4, rows), f32)
    by_device = pltpu.VMEM((steps, replicas, 4, rows), f32)
    spectrum = pltpu.VMEM((steps, pairs, 8, double), f32)
    taps_spectrum = pltpu.VMEM((steps, 8, double), f32)
    results = pl.pallas_call(
        functools.partial(kernel, steps, replicas, replicas * inputs.shape[0]),
        out_shape=(
            jax.ShapeDtypeStruct((rows, width), f32),
            jax.ShapeDtypeStruct((rows, width), f32),
            jax.ShapeDtypeStruct((width // replicas, rows), f32),
        ),
        in_specs=[anywhere] * 9,
        out_specs=(anywhere, anywhere, anywhere),
        scratch_shapes=[block, block, block, block, pltpu.VMEM((1, width), f32)]
        + [pltpu.VMEM((rows, double), bf16)] * 2
        + [pltpu.VMEM((double, rows), bf16)] * 2
        + [pltpu.VMEM((replicas, width // replicas, rows), f32), by_seq, by_seq]
        + [by_group, by_device, by_group, by_device]
        + [pltpu.VMEM((steps * pairs, 8, rows), f32), pltpu.VMEM((steps, 8, rows), f32)]
        + [taps_spectrum, spectrum, spectrum, spectrum, taps_spectrum]
        + [by_device, by_group, by_device, by_group, by_seq, by_seq]
        + [pltpu.VMEM((width // 8, 8, rows), f32), dma((9,))]
        + [dma((n,)) for n in [steps] * 2 + [devices] * 8 + [steps] * 2 + [3]],
        compiler_params=pltpu.CompilerParams(
            collective_id=0, has_side_effects=True, vmem_limit_bytes=60 * 1024 * 1024
        ),
    )(
        inputs[0], gate_values[0], out_grad[0], filter_taps, skip_gain[None, :],
        *[jnp.asarray(table) for table in tables],
    )
    input_part, gate_part, filter_part = pl.pallas_call(
        hand_over,
        out_shape=tuple(jax.ShapeDtypeStruct(part.shape, part.dtype) for part in results),
        in_specs=[anywhere] * 3,
        out_specs=(anywhere,) * 3,
        scratch_shapes=[dma((3,))],
        compiler_params=pltpu.CompilerParams(vmem_limit_bytes=60 * 1024 * 1024),
    )(*results)
    return input_part[None], gate_part[None], filter_part.T


def solution(mesh):
    placed = (P("dp", "seq", None), P("dp", "seq", None), P("dp", "seq", None), P("seq", None), P())
    steps, replicas = mesh.shape["seq"], mesh.shape["dp"]

    def either(inputs, gate_values, out_grad, filter_taps, skip_gain):
        rows, width = filter_taps.shape
        fits = width == 4 * steps * replicas and replicas % 2 == 0 and rows % 128 == 0 and steps <= 8
        if fits and inputs.shape[0] == 1:
            return fused(inputs, gate_values, out_grad, filter_taps, skip_gain, steps, replicas)
        return local(inputs, gate_values, out_grad, filter_taps, skip_gain)

    return jax.shard_map(
        either,
        mesh=mesh,
        in_specs=placed,
        out_specs=(P("dp", "seq", None), P("dp", "seq", None), P("seq", "dp")),
        check_vma=False,
    )
```

```python
import functools
import math

import jax
import jax.numpy as jnp
import ml_dtypes
import numpy as np
from jax import lax
from jax.experimental import pallas as pl
from jax.experimental.pallas import tpu as pltpu
from jax.sharding import PartitionSpec as P

first_radix = 32


def rotation(product, modulus, direction):
    fraction = (product % modulus).astype(jnp.float32) / modulus
    turned = 2.0 * math.pi * fraction
    return (jnp.cos(turned), direction * jnp.sin(turned))


def contract(formula, matrix, operand):
    return jnp.einsum(
        formula,
        matrix,
        operand,
        precision=lax.Precision.HIGHEST,
        preferred_element_type=jnp.float32,
    )


def complex_apply(formula, table_re, table_im, values_re, values_im):
    result_re = contract(formula, table_re, values_re) - contract(formula, table_im, values_im)
    result_im = contract(formula, table_re, values_im) + contract(formula, table_im, values_re)
    return (result_re, result_im)


def local_forward(values_re, values_im):
    pairs, rows, width = values_re.shape
    second = rows // first_radix
    values_re = values_re.reshape(pairs, first_radix, second, width)
    values_im = values_im.reshape(pairs, first_radix, second, width)
    outer = jnp.arange(first_radix, dtype=jnp.int32)
    inner = jnp.arange(second, dtype=jnp.int32)
    table_re, table_im = rotation(outer[:, None] * outer[None, :], first_radix, -1.0)
    section_re, section_im = complex_apply(
        "ca,mabx->mcbx", table_re, table_im, values_re, values_im
    )
    twist_re, twist_im = rotation(outer[:, None] * inner[None, :], rows, -1.0)
    twist_re = twist_re[None, :, :, None]
    twist_im = twist_im[None, :, :, None]
    turned_re = section_re * twist_re - section_im * twist_im
    turned_im = section_re * twist_im + section_im * twist_re
    table_re, table_im = rotation(inner[:, None] * inner[None, :], second, -1.0)
    return complex_apply("db,mcbx->mcdx", table_re, table_im, turned_re, turned_im)


def local_inverse(spec_re, spec_im):
    pairs, first, second, width = spec_re.shape
    rows = first * second
    outer = jnp.arange(first, dtype=jnp.int32)
    inner = jnp.arange(second, dtype=jnp.int32)
    table_re, table_im = rotation(inner[:, None] * inner[None, :], second, 1.0)
    section_re, section_im = complex_apply("bd,mcdx->mcbx", table_re, table_im, spec_re, spec_im)
    twist_re, twist_im = rotation(outer[:, None] * inner[None, :], rows, 1.0)
    twist_re = twist_re[None, :, :, None]
    twist_im = twist_im[None, :, :, None]
    turned_re = section_re * twist_re - section_im * twist_im
    turned_im = section_re * twist_im + section_im * twist_re
    table_re, table_im = rotation(outer[:, None] * outer[None, :], first, 1.0)
    result_re, result_im = complex_apply("ac,mcbx->mabx", table_re, table_im, turned_re, turned_im)
    return (result_re.reshape(pairs, rows, width), result_im.reshape(pairs, rows, width))


def frequency_labels():
    steps = lax.axis_size("seq")
    own = lax.axis_index("seq")
    local_labels = 2 * own + jnp.arange(2, dtype=jnp.int32)
    all_labels = jnp.arange(2 * steps, dtype=jnp.int32)
    return (local_labels, all_labels)


def forward_spectrum(signal):
    rows, width = signal.shape
    steps = lax.axis_size("seq")
    piece = rows // steps
    double = 2 * steps
    total = double * rows
    columns = lax.all_to_all(
        signal.reshape(1, rows, width), "seq", split_axis=1, concat_axis=0, tiled=True
    )
    block_index = jnp.arange(steps, dtype=jnp.int32)
    freq_index = jnp.arange(double, dtype=jnp.int32)
    table_re, table_im = rotation(freq_index[:, None] * block_index[None, :], double, -1.0)
    coarse_re = contract("kq,qrc->krc", table_re, columns)
    coarse_im = contract("kq,qrc->krc", table_im, columns)
    offsets = lax.axis_index("seq") * piece + jnp.arange(piece, dtype=jnp.int32)
    twist_re, twist_im = rotation(freq_index[:, None] * offsets[None, :], total, -1.0)
    twist_re = twist_re[:, :, None]
    twist_im = twist_im[:, :, None]
    turned_re = coarse_re * twist_re - coarse_im * twist_im
    turned_im = coarse_re * twist_im + coarse_im * twist_re
    moved = lax.all_to_all(
        jnp.stack([turned_re, turned_im]), "seq", split_axis=1, concat_axis=2, tiled=True
    )
    return local_forward(moved[0], moved[1])


def inverse_time(spec_re, spec_im, local_labels, all_labels):
    pairs, first, second, width = spec_re.shape
    rows = first * second
    steps = lax.axis_size("seq")
    double = 2 * steps
    total = double * rows
    time_re, time_im = local_inverse(spec_re, spec_im)
    positions = jnp.arange(rows, dtype=jnp.int32)
    twist_re, twist_im = rotation(local_labels[:, None] * positions[None, :], total, 1.0)
    twist_re = twist_re[:, :, None]
    twist_im = twist_im[:, :, None]
    turned_re = time_re * twist_re - time_im * twist_im
    turned_im = time_re * twist_im + time_im * twist_re
    moved = lax.all_to_all(
        jnp.stack([turned_re, turned_im]), "seq", split_axis=2, concat_axis=1, tiled=True
    )
    block_index = jnp.arange(steps, dtype=jnp.int32)
    table_re, table_im = rotation(block_index[:, None] * all_labels[None, :], double, 1.0)
    result_re = (
        contract("qk,krc->qrc", table_re, moved[0]) - contract("qk,krc->qrc", table_im, moved[1])
    ) / total
    result_im = (
        contract("qk,krc->qrc", table_re, moved[1]) + contract("qk,krc->qrc", table_im, moved[0])
    ) / total
    return (result_re, result_im)


def local(inputs, gate_values, out_grad, filter_taps, skip_gain):
    seq_input = inputs[0]
    seq_gate = gate_values[0]
    seq_grad = out_grad[0]
    rows, width = seq_input.shape
    replicas = lax.axis_size("dp")
    conv_grad = seq_grad * seq_gate
    spec_re, spec_im = forward_spectrum(
        jnp.concatenate([seq_input, conv_grad, filter_taps], axis=1)
    )
    filter_re = spec_re[..., 2 * width :]
    filter_im = spec_im[..., 2 * width :]
    input_re = spec_re[..., :width]
    input_im = spec_im[..., :width]
    grad_re = spec_re[..., width : 2 * width]
    grad_im = spec_im[..., width : 2 * width]
    conv_re = filter_re * input_re - filter_im * input_im
    conv_im = filter_re * input_im + filter_im * input_re
    corr_re = filter_re * grad_re + filter_im * grad_im
    corr_im = filter_re * grad_im - filter_im * grad_re
    taps_re = input_re * grad_re + input_im * grad_im
    taps_im = input_re * grad_im - input_im * grad_re
    packed_re = conv_re - corr_im
    packed_im = conv_im + corr_re
    local_labels, all_labels = frequency_labels()
    result_re, result_im = inverse_time(
        jnp.concatenate([packed_re, taps_re], axis=3),
        jnp.concatenate([packed_im, taps_im], axis=3),
        local_labels,
        all_labels,
    )
    results = jnp.concatenate([result_re, result_im[..., :width]], axis=2)
    timeline = lax.all_to_all(results, "seq", split_axis=0, concat_axis=1, tiled=True)[0]
    conv_time = timeline[:, :width]
    corr_time = timeline[:, timeline.shape[1] - width :]
    taps_time = timeline[:, width : timeline.shape[1] - width]
    taps_time = lax.psum_scatter(taps_time, "dp", scatter_dimension=1, tiled=True)
    gate_part = seq_grad * (conv_time + skip_gain[None, :] * seq_input)
    input_part = corr_time + skip_gain[None, :] * conv_grad
    length_total = rows * lax.axis_size("seq")
    batch_total = replicas * inputs.shape[0]
    filter_part = taps_time / math.sqrt(batch_total * length_total)
    return (input_part[None], gate_part[None], filter_part)


MESH = pl.DeviceIdType.MESH


def split_halves(table):
    high = table.astype(ml_dtypes.bfloat16)
    low = (table - high.astype(np.float64)).astype(ml_dtypes.bfloat16)
    return high, low


def block_tables(rows):
    double = 2 * rows
    place = np.arange(rows)
    turned = 2.0 * np.pi * ((place[:, None] * place[None, :]) % double) / double
    real = np.cos(turned)
    imag = -np.sin(turned)
    imag[:, 0] = 1.0 - 2.0 * (place % 2)
    forward = np.concatenate([real, imag], axis=1)
    weight = np.full((double, 1), 2.0 / double)
    weight[0] = weight[rows] = 1.0 / double
    inverse = forward.T * weight
    return split_halves(forward) + split_halves(inverse)


def dot3(values, high, low):
    top = values.astype(jnp.bfloat16)
    rest = (values - top.astype(jnp.float32)).astype(jnp.bfloat16)
    dot = functools.partial(jnp.dot, preferred_element_type=jnp.float32)
    return dot(top, high) + (dot(rest, high) + dot(top, low))


def kernel(
    steps, replicas, batch_total,
    in_any, gate_any, og_any, taps_any, skip_any, fh_any, fl_any, ih_any, il_any,
    ig_any, gg_any, fg_any,
    inp, gate, og, taps, skip, fh, fl, ih, il,
    tall, tsend, trecv, xsend, xrecv, gsend, grecv,
    rows8, trows8, spec_t, spec_x, spec_g, prod, tprod,
    csend, crecv, rsend, rrecv, bsend, brecv, merged,
    load_sem, tsend_sem, trecv_sem, xsend_sem, xrecv_sem, gsend_sem, grecv_sem,
    csend_sem, crecv_sem, rsend_sem, rrecv_sem, bsend_sem, brecv_sem, store_sem,
):
    devices = steps * replicas
    pairs = replicas // 2
    own_s = lax.axis_index("seq")
    own_d = lax.axis_index("dp")
    me = own_s * replicas + own_d
    group = own_d * steps + own_s
    rows, width = inp.shape
    lanes = 128
    half = 4

    barrier = pltpu.get_barrier_semaphore()

    def greet(i, carry):
        p = lax.rem(me + i, devices)
        pl.semaphore_signal(
            barrier, inc=1, device_id=(p // replicas, lax.rem(p, replicas)), device_id_type=MESH
        )
        return carry

    loads = [
        pltpu.make_async_copy(src, dst, load_sem.at[k])
        for k, (src, dst) in enumerate([
            (taps_any, taps), (in_any, inp), (og_any, og), (gate_any, gate), (skip_any, skip),
            (fh_any, fh), (fl_any, fl), (ih_any, ih), (il_any, il),
        ])
    ]
    for copy in loads:
        copy.start()
    lax.fori_loop(1, devices, greet, 0)

    def seq_copy(src, dst, src_sem, dst_sem, s, q):
        return pltpu.make_async_remote_copy(
            src_ref=src.at[s], dst_ref=dst.at[q], send_sem=src_sem.at[s],
            recv_sem=dst_sem.at[q], device_id=(s, own_d), device_id_type=MESH,
        )

    def out_copy(src, dst, src_sem, dst_sem, p, q):
        s, d = p // replicas, lax.rem(p, replicas)
        return pltpu.make_async_remote_copy(
            src_ref=src.at[d * steps + s], dst_ref=dst.at[q // replicas, lax.rem(q, replicas)],
            send_sem=src_sem.at[p], recv_sem=dst_sem.at[q], device_id=(s, d), device_id_type=MESH,
        )

    def back_copy(src, dst, src_sem, dst_sem, p, q):
        s, d = p // replicas, lax.rem(p, replicas)
        return pltpu.make_async_remote_copy(
            src_ref=src.at[s, d], dst_ref=dst.at[lax.rem(q, replicas) * steps + q // replicas],
            send_sem=src_sem.at[p], recv_sem=dst_sem.at[q], device_id=(s, d), device_id_type=MESH,
        )

    def over_seq(use):
        def body(i, carry):
            use(lax.rem(own_s + i, steps))
            return carry

        lax.fori_loop(1, steps, body, 0)

    def over_all(use):
        def body(i, carry):
            use(lax.rem(me + stride * i, devices))
            return carry

        lax.fori_loop(1, devices, body, 0)

    t_refs = (tsend, trecv, tsend_sem, trecv_sem)
    x_refs = (xsend, xrecv, xsend_sem, xrecv_sem)
    g_refs = (gsend, grecv, gsend_sem, grecv_sem)
    c_refs = (csend, crecv, csend_sem, crecv_sem)
    r_refs = (rsend, rrecv, rsend_sem, rrecv_sem)
    b_refs = (bsend, brecv, bsend_sem, brecv_sem)

    def to_channels(values, ref):
        turned = values.T
        for k in range(width // half):
            ref[k] = turned[half * k : half * k + half]

    loads[0].wait()
    tall[...] = taps[...].T.reshape(replicas, steps * half, rows)
    mine = tall[own_d]
    for k in range(steps):
        tsend[k] = mine[half * k : half * k + half]
    loads[1].wait()
    to_channels(inp[...], xsend)
    pl.semaphore_wait(barrier, devices - 1)
    over_seq(lambda s: seq_copy(*t_refs, s, own_s).start())
    over_all(lambda p: out_copy(*x_refs, p, me).start())
    loads[2].wait()
    loads[3].wait()
    gate[...] = og[...] * gate[...]
    to_channels(gate[...], gsend)
    over_all(lambda p: out_copy(*g_refs, p, me).start())
    trecv[own_s] = tsend[own_s]
    xrecv[own_s, own_d] = xsend[group]
    grecv[own_s, own_d] = gsend[group]
    for copy in loads[4:]:
        copy.wait()

    lane = lax.broadcasted_iota(jnp.int32, (8, lanes), 1)
    sign = (1 - 2 * lax.rem(lane, 2)).astype(jnp.float32)

    def forward(ref, spec):
        for s in range(steps):
            for d in range(replicas):
                at = half * (d % 2)
                rows8[s * pairs + d // 2, at : at + half] = ref[s, d]
        spec[...] = dot3(rows8[...].reshape(steps * pairs * 8, rows), fh[...], fl[...]).reshape(
            steps, pairs, 8, 2 * rows
        )

    def backward(ref):
        result = dot3(prod[...].reshape(steps * pairs * 8, 2 * rows), ih[...], il[...])
        for s in range(steps):
            for d in range(replicas):
                at = half * (replicas * s + d)
                ref[s, d] = result[at : at + half]

    def slices(c):
        re_at = pl.ds(pl.multiple_of(c * lanes, lanes), lanes)
        im_at = pl.ds(pl.multiple_of(rows + c * lanes, lanes), lanes)
        return re_at, im_at, (lane + c * lanes) == 0

    def shifted(re, im, first):
        out_re = [re[0]] + [re[j] + sign * re[j - 1] for j in range(1, steps)]
        out_im = [im[0]] + [im[j] + sign * im[j - 1] for j in range(1, steps)]
        out_re2 = [jnp.where(first, b, a) for a, b in zip(out_re, out_im)]
        return out_re, [jnp.where(first, 0.0, b) for b in out_im], out_re2

    def add(total, term):
        return term if total is None else total + term

    def filter_blocks(re_at, im_at, first):
        return shifted(
            [spec_t[j, :, re_at] for j in range(steps)], [spec_t[j, :, im_at] for j in range(steps)], first
        )

    def blocks(spec, k, at):
        return [spec[j, k, :, at] for j in range(steps)]

    def convolve(c, carry):
        re_at, im_at, first = slices(c)
        h_re, h_im, h_re2 = filter_blocks(re_at, im_at, first)
        for k in range(pairs):
            x_re, x_im = blocks(spec_x, k, re_at), blocks(spec_x, k, im_at)
            for u in range(steps):
                re, im = None, None
                for v in range(u + 1):
                    j = u - v
                    re = add(re, h_re[j] * x_re[v] - h_im[j] * x_im[v])
                    im = add(im, h_re2[j] * x_im[v] + h_im[j] * x_re[v])
                prod[u, k, :, re_at] = re
                prod[u, k, :, im_at] = im
        return carry

    def correlate(c, carry):
        re_at, im_at, first = slices(c)
        h_re, h_im, h_re2 = filter_blocks(re_at, im_at, first)
        for k in range(pairs):
            g_re, g_im = blocks(spec_g, k, re_at), blocks(spec_g, k, im_at)
            for u in range(steps):
                re, im = None, None
                for v in range(u, steps):
                    j = v - u
                    re = add(re, h_re[j] * g_re[v] + h_im[j] * g_im[v])
                    im = add(im, h_re2[j] * g_im[v] - h_im[j] * g_re[v])
                prod[u, k, :, re_at] = re
                prod[u, k, :, im_at] = im
        return carry

    def correlate_taps(c, carry):
        re_at, im_at, first = slices(c)
        sums_re, sums_im = [None] * steps, [None] * steps
        for k in range(pairs):
            x_re, x_im, x_re2 = shifted(blocks(spec_x, k, re_at), blocks(spec_x, k, im_at), first)
            g_re, g_im = blocks(spec_g, k, re_at), blocks(spec_g, k, im_at)
            for u in range(steps):
                for v in range(u, steps):
                    j = v - u
                    sums_re[u] = add(sums_re[u], g_re[v] * x_re[j] + g_im[v] * x_im[j])
                    sums_im[u] = add(sums_im[u], g_im[v] * x_re2[j] - g_re[v] * x_im[j])
        for u in range(steps):
            tprod[u, :, re_at] = sums_re[u] + pltpu.roll(sums_re[u], half, 0)
            tprod[u, :, im_at] = sums_im[u] + pltpu.roll(sums_im[u], half, 0)
        return carry

    def to_positions(ref):
        for k in range(width // half):
            at = half * (k % 2)
            merged[k // 2, at : at + half] = ref[k]
        return merged[...].reshape(width, rows).T

    over_seq(lambda s: seq_copy(*t_refs, s, s).wait_recv())
    for k in range(steps):
        trows8[k, :half] = trecv[k]
        trows8[k, half:] = trecv[k]
    spec_t[...] = dot3(trows8[...].reshape(steps * 8, rows), fh[...], fl[...]).reshape(steps, 8, 2 * rows)

    over_all(lambda p: out_copy(*x_refs, p, p).wait_recv())
    forward(xrecv, spec_x)
    lax.fori_loop(0, rows // lanes, convolve, 0)
    backward(csend)
    over_all(lambda p: back_copy(*c_refs, p, me).start())

    over_all(lambda p: out_copy(*g_refs, p, p).wait_recv())
    forward(grecv, spec_g)
    lax.fori_loop(0, rows // lanes, correlate, 0)
    backward(rsend)
    over_all(lambda p: back_copy(*r_refs, p, me).start())

    lax.fori_loop(0, rows // lanes, correlate_taps, 0)
    folded = dot3(tprod[...].reshape(steps * 8, 2 * rows), ih[...], il[...])
    for k in range(steps):
        bsend[k] = folded[8 * k : 8 * k + half]
    over_seq(lambda s: seq_copy(*b_refs, s, own_s).start())

    crecv[group] = csend[own_s, own_d]
    rrecv[group] = rsend[own_s, own_d]
    brecv[own_s] = bsend[own_s]

    over_all(lambda p: back_copy(*c_refs, p, p).wait_recv())
    gain = skip[...]
    og[...] = og[...] * (to_positions(crecv) + gain * inp[...])
    stores = [
        pltpu.make_async_copy(src, dst, store_sem.at[k])
        for k, (src, dst) in enumerate([(og, gg_any), (gate, ig_any), (tall.at[0], fg_any)])
    ]
    stores[0].start()
    over_all(lambda p: back_copy(*r_refs, p, p).wait_recv())
    gate[...] = to_positions(rrecv) + gain * gate[...]
    stores[1].start()
    over_seq(lambda s: seq_copy(*b_refs, s, s).wait_recv())
    scale = 1.0 / math.sqrt(batch_total * rows * steps)
    tall[0] = scale * jnp.concatenate([brecv[k] for k in range(steps)], axis=0)
    stores[2].start()

    over_seq(lambda s: seq_copy(*t_refs, s, s).wait_send())
    over_seq(lambda s: seq_copy(*b_refs, s, s).wait_send())
    over_all(lambda p: out_copy(*x_refs, p, p).wait_send())
    over_all(lambda p: out_copy(*g_refs, p, p).wait_send())
    over_all(lambda p: back_copy(*c_refs, p, p).wait_send())
    over_all(lambda p: back_copy(*r_refs, p, p).wait_send())
    for copy in stores:
        copy.wait()


def hand_over(*refs):
    reads = [pltpu.make_async_copy(refs[k], refs[6 + k], refs[9].at[k]) for k in range(3)]
    writes = [pltpu.make_async_copy(refs[6 + k], refs[3 + k], refs[9].at[3 + k]) for k in range(3)]
    for copy in reads:
        copy.start()
    for read, write in zip(reads, writes):
        read.wait()
        write.start()
    for copy in writes:
        copy.wait()


stride = 1


def fused(inputs, gate_values, out_grad, filter_taps, skip_gain, steps, replicas):
    rows, width = filter_taps.shape
    devices = steps * replicas
    pairs = replicas // 2
    double = 2 * rows
    tables = block_tables(rows)
    f32, bf16 = jnp.float32, jnp.bfloat16
    dma = pltpu.SemaphoreType.DMA
    anywhere = pl.BlockSpec(memory_space=pltpu.HBM)
    block = pltpu.VMEM((rows, width), f32)
    by_seq = pltpu.VMEM((steps, 4, rows), f32)
    by_group = pltpu.VMEM((devices, 4, rows), f32)
    by_device = pltpu.VMEM((steps, replicas, 4, rows), f32)
    spectrum = pltpu.VMEM((steps, pairs, 8, double), f32)
    taps_spectrum = pltpu.VMEM((steps, 8, double), f32)
    results = pl.pallas_call(
        functools.partial(kernel, steps, replicas, replicas * inputs.shape[0]),
        out_shape=(
            jax.ShapeDtypeStruct((rows, width), f32),
            jax.ShapeDtypeStruct((rows, width), f32),
            jax.ShapeDtypeStruct((width // replicas, rows), f32),
        ),
        in_specs=[anywhere] * 9,
        out_specs=(anywhere, anywhere, anywhere),
        scratch_shapes=[block, block, block, block, pltpu.VMEM((1, width), f32)]
        + [pltpu.VMEM((rows, double), bf16)] * 2
        + [pltpu.VMEM((double, rows), bf16)] * 2
        + [pltpu.VMEM((replicas, width // replicas, rows), f32), by_seq, by_seq]
        + [by_group, by_device, by_group, by_device]
        + [pltpu.VMEM((steps * pairs, 8, rows), f32), pltpu.VMEM((steps, 8, rows), f32)]
        + [taps_spectrum, spectrum, spectrum, spectrum, taps_spectrum]
        + [by_device, by_group, by_device, by_group, by_seq, by_seq]
        + [pltpu.VMEM((width // 8, 8, rows), f32), dma((9,))]
        + [dma((n,)) for n in [steps] * 2 + [devices] * 8 + [steps] * 2 + [3]],
        compiler_params=pltpu.CompilerParams(
            collective_id=0, has_side_effects=True, vmem_limit_bytes=60 * 1024 * 1024
        ),
    )(
        inputs[0], gate_values[0], out_grad[0], filter_taps, skip_gain[None, :],
        *[jnp.asarray(table) for table in tables],
    )
    input_part, gate_part, filter_part = pl.pallas_call(
        hand_over,
        out_shape=tuple(jax.ShapeDtypeStruct(part.shape, part.dtype) for part in results),
        in_specs=[anywhere] * 3,
        out_specs=(anywhere,) * 3,
        scratch_shapes=[pltpu.VMEM(part.shape, part.dtype) for part in results] + [dma((6,))],
        compiler_params=pltpu.CompilerParams(vmem_limit_bytes=60 * 1024 * 1024),
    )(*results)
    return input_part[None], gate_part[None], filter_part.T


def solution(mesh):
    placed = (P("dp", "seq", None), P("dp", "seq", None), P("dp", "seq", None), P("seq", None), P())
    steps, replicas = mesh.shape["seq"], mesh.shape["dp"]

    def either(inputs, gate_values, out_grad, filter_taps, skip_gain):
        rows, width = filter_taps.shape
        fits = width == 4 * steps * replicas and replicas % 2 == 0 and rows % 128 == 0 and steps <= 8
        if fits and inputs.shape[0] == 1:
            return fused(inputs, gate_values, out_grad, filter_taps, skip_gain, steps, replicas)
        return local(inputs, gate_values, out_grad, filter_taps, skip_gain)

    return jax.shard_map(
        either,
        mesh=mesh,
        in_specs=placed,
        out_specs=(P("dp", "seq", None), P("dp", "seq", None), P("seq", "dp")),
        check_vma=False,
    )
```

```python
import functools
import math

import jax
import jax.numpy as jnp
import ml_dtypes
import numpy as np
from jax import lax
from jax.experimental import pallas as pl
from jax.experimental.pallas import tpu as pltpu
from jax.sharding import PartitionSpec as P

first_radix = 32


def rotation(product, modulus, direction):
    fraction = (product % modulus).astype(jnp.float32) / modulus
    turned = 2.0 * math.pi * fraction
    return (jnp.cos(turned), direction * jnp.sin(turned))


def contract(formula, matrix, operand):
    return jnp.einsum(
        formula,
        matrix,
        operand,
        precision=lax.Precision.HIGHEST,
        preferred_element_type=jnp.float32,
    )


def complex_apply(formula, table_re, table_im, values_re, values_im):
    result_re = contract(formula, table_re, values_re) - contract(formula, table_im, values_im)
    result_im = contract(formula, table_re, values_im) + contract(formula, table_im, values_re)
    return (result_re, result_im)


def local_forward(values_re, values_im):
    pairs, rows, width = values_re.shape
    second = rows // first_radix
    values_re = values_re.reshape(pairs, first_radix, second, width)
    values_im = values_im.reshape(pairs, first_radix, second, width)
    outer = jnp.arange(first_radix, dtype=jnp.int32)
    inner = jnp.arange(second, dtype=jnp.int32)
    table_re, table_im = rotation(outer[:, None] * outer[None, :], first_radix, -1.0)
    section_re, section_im = complex_apply(
        "ca,mabx->mcbx", table_re, table_im, values_re, values_im
    )
    twist_re, twist_im = rotation(outer[:, None] * inner[None, :], rows, -1.0)
    twist_re = twist_re[None, :, :, None]
    twist_im = twist_im[None, :, :, None]
    turned_re = section_re * twist_re - section_im * twist_im
    turned_im = section_re * twist_im + section_im * twist_re
    table_re, table_im = rotation(inner[:, None] * inner[None, :], second, -1.0)
    return complex_apply("db,mcbx->mcdx", table_re, table_im, turned_re, turned_im)


def local_inverse(spec_re, spec_im):
    pairs, first, second, width = spec_re.shape
    rows = first * second
    outer = jnp.arange(first, dtype=jnp.int32)
    inner = jnp.arange(second, dtype=jnp.int32)
    table_re, table_im = rotation(inner[:, None] * inner[None, :], second, 1.0)
    section_re, section_im = complex_apply("bd,mcdx->mcbx", table_re, table_im, spec_re, spec_im)
    twist_re, twist_im = rotation(outer[:, None] * inner[None, :], rows, 1.0)
    twist_re = twist_re[None, :, :, None]
    twist_im = twist_im[None, :, :, None]
    turned_re = section_re * twist_re - section_im * twist_im
    turned_im = section_re * twist_im + section_im * twist_re
    table_re, table_im = rotation(outer[:, None] * outer[None, :], first, 1.0)
    result_re, result_im = complex_apply("ac,mcbx->mabx", table_re, table_im, turned_re, turned_im)
    return (result_re.reshape(pairs, rows, width), result_im.reshape(pairs, rows, width))


def frequency_labels():
    steps = lax.axis_size("seq")
    own = lax.axis_index("seq")
    local_labels = 2 * own + jnp.arange(2, dtype=jnp.int32)
    all_labels = jnp.arange(2 * steps, dtype=jnp.int32)
    return (local_labels, all_labels)


def forward_spectrum(signal):
    rows, width = signal.shape
    steps = lax.axis_size("seq")
    piece = rows // steps
    double = 2 * steps
    total = double * rows
    columns = lax.all_to_all(
        signal.reshape(1, rows, width), "seq", split_axis=1, concat_axis=0, tiled=True
    )
    block_index = jnp.arange(steps, dtype=jnp.int32)
    freq_index = jnp.arange(double, dtype=jnp.int32)
    table_re, table_im = rotation(freq_index[:, None] * block_index[None, :], double, -1.0)
    coarse_re = contract("kq,qrc->krc", table_re, columns)
    coarse_im = contract("kq,qrc->krc", table_im, columns)
    offsets = lax.axis_index("seq") * piece + jnp.arange(piece, dtype=jnp.int32)
    twist_re, twist_im = rotation(freq_index[:, None] * offsets[None, :], total, -1.0)
    twist_re = twist_re[:, :, None]
    twist_im = twist_im[:, :, None]
    turned_re = coarse_re * twist_re - coarse_im * twist_im
    turned_im = coarse_re * twist_im + coarse_im * twist_re
    moved = lax.all_to_all(
        jnp.stack([turned_re, turned_im]), "seq", split_axis=1, concat_axis=2, tiled=True
    )
    return local_forward(moved[0], moved[1])


def inverse_time(spec_re, spec_im, local_labels, all_labels):
    pairs, first, second, width = spec_re.shape
    rows = first * second
    steps = lax.axis_size("seq")
    double = 2 * steps
    total = double * rows
    time_re, time_im = local_inverse(spec_re, spec_im)
    positions = jnp.arange(rows, dtype=jnp.int32)
    twist_re, twist_im = rotation(local_labels[:, None] * positions[None, :], total, 1.0)
    twist_re = twist_re[:, :, None]
    twist_im = twist_im[:, :, None]
    turned_re = time_re * twist_re - time_im * twist_im
    turned_im = time_re * twist_im + time_im * twist_re
    moved = lax.all_to_all(
        jnp.stack([turned_re, turned_im]), "seq", split_axis=2, concat_axis=1, tiled=True
    )
    block_index = jnp.arange(steps, dtype=jnp.int32)
    table_re, table_im = rotation(block_index[:, None] * all_labels[None, :], double, 1.0)
    result_re = (
        contract("qk,krc->qrc", table_re, moved[0]) - contract("qk,krc->qrc", table_im, moved[1])
    ) / total
    result_im = (
        contract("qk,krc->qrc", table_re, moved[1]) + contract("qk,krc->qrc", table_im, moved[0])
    ) / total
    return (result_re, result_im)


def local(inputs, gate_values, out_grad, filter_taps, skip_gain):
    seq_input = inputs[0]
    seq_gate = gate_values[0]
    seq_grad = out_grad[0]
    rows, width = seq_input.shape
    replicas = lax.axis_size("dp")
    conv_grad = seq_grad * seq_gate
    spec_re, spec_im = forward_spectrum(
        jnp.concatenate([seq_input, conv_grad, filter_taps], axis=1)
    )
    filter_re = spec_re[..., 2 * width :]
    filter_im = spec_im[..., 2 * width :]
    input_re = spec_re[..., :width]
    input_im = spec_im[..., :width]
    grad_re = spec_re[..., width : 2 * width]
    grad_im = spec_im[..., width : 2 * width]
    conv_re = filter_re * input_re - filter_im * input_im
    conv_im = filter_re * input_im + filter_im * input_re
    corr_re = filter_re * grad_re + filter_im * grad_im
    corr_im = filter_re * grad_im - filter_im * grad_re
    taps_re = input_re * grad_re + input_im * grad_im
    taps_im = input_re * grad_im - input_im * grad_re
    packed_re = conv_re - corr_im
    packed_im = conv_im + corr_re
    local_labels, all_labels = frequency_labels()
    result_re, result_im = inverse_time(
        jnp.concatenate([packed_re, taps_re], axis=3),
        jnp.concatenate([packed_im, taps_im], axis=3),
        local_labels,
        all_labels,
    )
    results = jnp.concatenate([result_re, result_im[..., :width]], axis=2)
    timeline = lax.all_to_all(results, "seq", split_axis=0, concat_axis=1, tiled=True)[0]
    conv_time = timeline[:, :width]
    corr_time = timeline[:, timeline.shape[1] - width :]
    taps_time = timeline[:, width : timeline.shape[1] - width]
    taps_time = lax.psum_scatter(taps_time, "dp", scatter_dimension=1, tiled=True)
    gate_part = seq_grad * (conv_time + skip_gain[None, :] * seq_input)
    input_part = corr_time + skip_gain[None, :] * conv_grad
    length_total = rows * lax.axis_size("seq")
    batch_total = replicas * inputs.shape[0]
    filter_part = taps_time / math.sqrt(batch_total * length_total)
    return (input_part[None], gate_part[None], filter_part)


MESH = pl.DeviceIdType.MESH


def split_halves(table):
    high = table.astype(ml_dtypes.bfloat16)
    low = (table - high.astype(np.float64)).astype(ml_dtypes.bfloat16)
    return high, low


def block_tables(rows):
    double = 2 * rows
    place = np.arange(rows)
    turned = 2.0 * np.pi * ((place[:, None] * place[None, :]) % double) / double
    real = np.cos(turned)
    imag = -np.sin(turned)
    imag[:, 0] = 1.0 - 2.0 * (place % 2)
    forward = np.concatenate([real, imag], axis=1)
    weight = np.full((double, 1), 2.0 / double)
    weight[0] = weight[rows] = 1.0 / double
    inverse = forward.T * weight
    return split_halves(forward) + split_halves(inverse)


def dot3(values, high, low):
    top = values.astype(jnp.bfloat16)
    rest = (values - top.astype(jnp.float32)).astype(jnp.bfloat16)
    dot = functools.partial(jnp.dot, preferred_element_type=jnp.float32)
    return dot(top, high) + (dot(rest, high) + dot(top, low))


def kernel(
    steps, replicas, batch_total,
    in_any, gate_any, og_any, taps_any, skip_any, fh_any, fl_any, ih_any, il_any,
    ig_any, gg_any, fg_any,
    inp, gate, og, taps, skip, fh, fl, ih, il,
    tall, tsend, trecv, xsend, xrecv, gsend, grecv,
    rows8, trows8, spec_t, spec_x, spec_g, prod, tprod,
    csend, crecv, rsend, rrecv, bsend, brecv, merged,
    load_sem, tsend_sem, trecv_sem, xsend_sem, xrecv_sem, gsend_sem, grecv_sem,
    csend_sem, crecv_sem, rsend_sem, rrecv_sem, bsend_sem, brecv_sem, store_sem,
):
    devices = steps * replicas
    pairs = replicas // 2
    own_s = lax.axis_index("seq")
    own_d = lax.axis_index("dp")
    me = own_s * replicas + own_d
    group = own_d * steps + own_s
    rows, width = inp.shape
    lanes = 128
    half = 4

    barrier = pltpu.get_barrier_semaphore()

    def greet(i, carry):
        p = lax.rem(me + i, devices)
        pl.semaphore_signal(
            barrier, inc=1, device_id=(p // replicas, lax.rem(p, replicas)), device_id_type=MESH
        )
        return carry

    loads = [
        pltpu.make_async_copy(src, dst, load_sem.at[k])
        for k, (src, dst) in enumerate([
            (taps_any, taps), (in_any, inp), (og_any, og), (gate_any, gate), (skip_any, skip),
            (fh_any, fh), (fl_any, fl), (ih_any, ih), (il_any, il),
        ])
    ]
    lax.fori_loop(1, devices, greet, 0)
    for copy in loads:
        copy.start()

    def seq_copy(src, dst, src_sem, dst_sem, s, q):
        return pltpu.make_async_remote_copy(
            src_ref=src.at[s], dst_ref=dst.at[q], send_sem=src_sem.at[s],
            recv_sem=dst_sem.at[q], device_id=(s, own_d), device_id_type=MESH,
        )

    def out_copy(src, dst, src_sem, dst_sem, p, q):
        s, d = p // replicas, lax.rem(p, replicas)
        return pltpu.make_async_remote_copy(
            src_ref=src.at[d * steps + s], dst_ref=dst.at[q // replicas, lax.rem(q, replicas)],
            send_sem=src_sem.at[p], recv_sem=dst_sem.at[q], device_id=(s, d), device_id_type=MESH,
        )

    def back_copy(src, dst, src_sem, dst_sem, p, q):
        s, d = p // replicas, lax.rem(p, replicas)
        return pltpu.make_async_remote_copy(
            src_ref=src.at[s, d], dst_ref=dst.at[lax.rem(q, replicas) * steps + q // replicas],
            send_sem=src_sem.at[p], recv_sem=dst_sem.at[q], device_id=(s, d), device_id_type=MESH,
        )

    def over_seq(use):
        def body(i, carry):
            use(lax.rem(own_s + i, steps))
            return carry

        lax.fori_loop(1, steps, body, 0)

    def over_all(use):
        def body(i, carry):
            use(lax.rem(me + stride * i, devices))
            return carry

        lax.fori_loop(1, devices, body, 0)

    t_refs = (tsend, trecv, tsend_sem, trecv_sem)
    x_refs = (xsend, xrecv, xsend_sem, xrecv_sem)
    g_refs = (gsend, grecv, gsend_sem, grecv_sem)
    c_refs = (csend, crecv, csend_sem, crecv_sem)
    r_refs = (rsend, rrecv, rsend_sem, rrecv_sem)
    b_refs = (bsend, brecv, bsend_sem, brecv_sem)

    def to_channels(values, ref):
        turned = values.T
        for k in range(width // half):
            ref[k] = turned[half * k : half * k + half]

    loads[0].wait()
    tall[...] = taps[...].T.reshape(replicas, steps * half, rows)
    mine = tall[own_d]
    for k in range(steps):
        tsend[k] = mine[half * k : half * k + half]
    loads[1].wait()
    to_channels(inp[...], xsend)
    pl.semaphore_wait(barrier, devices - 1)
    over_seq(lambda s: seq_copy(*t_refs, s, own_s).start())
    over_all(lambda p: out_copy(*x_refs, p, me).start())
    loads[2].wait()
    loads[3].wait()
    gate[...] = og[...] * gate[...]
    to_channels(gate[...], gsend)
    over_all(lambda p: out_copy(*g_refs, p, me).start())
    trecv[own_s] = tsend[own_s]
    xrecv[own_s, own_d] = xsend[group]
    grecv[own_s, own_d] = gsend[group]
    for copy in loads[4:]:
        copy.wait()

    lane = lax.broadcasted_iota(jnp.int32, (8, lanes), 1)
    sign = (1 - 2 * lax.rem(lane, 2)).astype(jnp.float32)

    def forward(ref, spec):
        for s in range(steps):
            for d in range(replicas):
                at = half * (d % 2)
                rows8[s * pairs + d // 2, at : at + half] = ref[s, d]
        spec[...] = dot3(rows8[...].reshape(steps * pairs * 8, rows), fh[...], fl[...]).reshape(
            steps, pairs, 8, 2 * rows
        )

    def backward(ref):
        result = dot3(prod[...].reshape(steps * pairs * 8, 2 * rows), ih[...], il[...])
        for s in range(steps):
            for d in range(replicas):
                at = half * (replicas * s + d)
                ref[s, d] = result[at : at + half]

    def slices(c):
        re_at = pl.ds(pl.multiple_of(c * lanes, lanes), lanes)
        im_at = pl.ds(pl.multiple_of(rows + c * lanes, lanes), lanes)
        return re_at, im_at, (lane + c * lanes) == 0

    def shifted(re, im, first):
        out_re = [re[0]] + [re[j] + sign * re[j - 1] for j in range(1, steps)]
        out_im = [im[0]] + [im[j] + sign * im[j - 1] for j in range(1, steps)]
        out_re2 = [jnp.where(first, b, a) for a, b in zip(out_re, out_im)]
        return out_re, [jnp.where(first, 0.0, b) for b in out_im], out_re2

    def add(total, term):
        return term if total is None else total + term

    def filter_blocks(re_at, im_at, first):
        return shifted(
            [spec_t[j, :, re_at] for j in range(steps)], [spec_t[j, :, im_at] for j in range(steps)], first
        )

    def blocks(spec, k, at):
        return [spec[j, k, :, at] for j in range(steps)]

    def convolve(c, carry):
        re_at, im_at, first = slices(c)
        h_re, h_im, h_re2 = filter_blocks(re_at, im_at, first)
        for k in range(pairs):
            x_re, x_im = blocks(spec_x, k, re_at), blocks(spec_x, k, im_at)
            for u in range(steps):
                re, im = None, None
                for v in range(u + 1):
                    j = u - v
                    re = add(re, h_re[j] * x_re[v] - h_im[j] * x_im[v])
                    im = add(im, h_re2[j] * x_im[v] + h_im[j] * x_re[v])
                prod[u, k, :, re_at] = re
                prod[u, k, :, im_at] = im
        return carry

    def correlate(c, carry):
        re_at, im_at, first = slices(c)
        h_re, h_im, h_re2 = filter_blocks(re_at, im_at, first)
        for k in range(pairs):
            g_re, g_im = blocks(spec_g, k, re_at), blocks(spec_g, k, im_at)
            for u in range(steps):
                re, im = None, None
                for v in range(u, steps):
                    j = v - u
                    re = add(re, h_re[j] * g_re[v] + h_im[j] * g_im[v])
                    im = add(im, h_re2[j] * g_im[v] - h_im[j] * g_re[v])
                prod[u, k, :, re_at] = re
                prod[u, k, :, im_at] = im
        return carry

    def correlate_taps(c, carry):
        re_at, im_at, first = slices(c)
        sums_re, sums_im = [None] * steps, [None] * steps
        for k in range(pairs):
            x_re, x_im, x_re2 = shifted(blocks(spec_x, k, re_at), blocks(spec_x, k, im_at), first)
            g_re, g_im = blocks(spec_g, k, re_at), blocks(spec_g, k, im_at)
            for u in range(steps):
                for v in range(u, steps):
                    j = v - u
                    sums_re[u] = add(sums_re[u], g_re[v] * x_re[j] + g_im[v] * x_im[j])
                    sums_im[u] = add(sums_im[u], g_im[v] * x_re2[j] - g_re[v] * x_im[j])
        for u in range(steps):
            tprod[u, :, re_at] = sums_re[u] + pltpu.roll(sums_re[u], half, 0)
            tprod[u, :, im_at] = sums_im[u] + pltpu.roll(sums_im[u], half, 0)
        return carry

    def to_positions(ref):
        for k in range(width // half):
            at = half * (k % 2)
            merged[k // 2, at : at + half] = ref[k]
        return merged[...].reshape(width, rows).T

    over_seq(lambda s: seq_copy(*t_refs, s, s).wait_recv())
    for k in range(steps):
        trows8[k, :half] = trecv[k]
        trows8[k, half:] = trecv[k]
    spec_t[...] = dot3(trows8[...].reshape(steps * 8, rows), fh[...], fl[...]).reshape(steps, 8, 2 * rows)

    over_all(lambda p: out_copy(*x_refs, p, p).wait_recv())
    forward(xrecv, spec_x)
    lax.fori_loop(0, rows // lanes, convolve, 0)
    backward(csend)
    over_all(lambda p: back_copy(*c_refs, p, me).start())

    over_all(lambda p: out_copy(*g_refs, p, p).wait_recv())
    forward(grecv, spec_g)
    lax.fori_loop(0, rows // lanes, correlate, 0)
    backward(rsend)
    over_all(lambda p: back_copy(*r_refs, p, me).start())

    lax.fori_loop(0, rows // lanes, correlate_taps, 0)
    folded = dot3(tprod[...].reshape(steps * 8, 2 * rows), ih[...], il[...])
    for k in range(steps):
        bsend[k] = folded[8 * k : 8 * k + half]
    over_seq(lambda s: seq_copy(*b_refs, s, own_s).start())

    crecv[group] = csend[own_s, own_d]
    rrecv[group] = rsend[own_s, own_d]
    brecv[own_s] = bsend[own_s]
    over_seq(lambda s: seq_copy(*t_refs, s, s).wait_send())
    over_all(lambda p: out_copy(*x_refs, p, p).wait_send())
    over_all(lambda p: out_copy(*g_refs, p, p).wait_send())

    over_all(lambda p: back_copy(*c_refs, p, p).wait_recv())
    gain = skip[...]
    og[...] = og[...] * (to_positions(crecv) + gain * inp[...])
    stores = [
        pltpu.make_async_copy(src, dst, store_sem.at[k])
        for k, (src, dst) in enumerate([(og, gg_any), (gate, ig_any), (tall.at[0], fg_any)])
    ]
    stores[0].start()
    over_all(lambda p: back_copy(*c_refs, p, p).wait_send())
    over_all(lambda p: back_copy(*r_refs, p, p).wait_recv())
    gate[...] = to_positions(rrecv) + gain * gate[...]
    stores[1].start()
    over_seq(lambda s: seq_copy(*b_refs, s, s).wait_recv())
    scale = 1.0 / math.sqrt(batch_total * rows * steps)
    tall[0] = scale * jnp.concatenate([brecv[k] for k in range(steps)], axis=0)
    stores[2].start()

    over_seq(lambda s: seq_copy(*b_refs, s, s).wait_send())
    over_all(lambda p: back_copy(*r_refs, p, p).wait_send())
    for copy in stores:
        copy.wait()


def hand_over(*refs):
    reads = [pltpu.make_async_copy(refs[k], refs[6 + k], refs[9].at[k]) for k in range(3)]
    writes = [pltpu.make_async_copy(refs[6 + k], refs[3 + k], refs[9].at[3 + k]) for k in range(3)]
    for copy in reads:
        copy.start()
    for read, write in zip(reads, writes):
        read.wait()
        write.start()
    for copy in writes:
        copy.wait()


stride = 1


def fused(inputs, gate_values, out_grad, filter_taps, skip_gain, steps, replicas):
    rows, width = filter_taps.shape
    devices = steps * replicas
    pairs = replicas // 2
    double = 2 * rows
    tables = block_tables(rows)
    f32, bf16 = jnp.float32, jnp.bfloat16
    dma = pltpu.SemaphoreType.DMA
    anywhere = pl.BlockSpec(memory_space=pltpu.HBM)
    block = pltpu.VMEM((rows, width), f32)
    by_seq = pltpu.VMEM((steps, 4, rows), f32)
    by_group = pltpu.VMEM((devices, 4, rows), f32)
    by_device = pltpu.VMEM((steps, replicas, 4, rows), f32)
    spectrum = pltpu.VMEM((steps, pairs, 8, double), f32)
    taps_spectrum = pltpu.VMEM((steps, 8, double), f32)
    results = pl.pallas_call(
        functools.partial(kernel, steps, replicas, replicas * inputs.shape[0]),
        out_shape=(
            jax.ShapeDtypeStruct((rows, width), f32),
            jax.ShapeDtypeStruct((rows, width), f32),
            jax.ShapeDtypeStruct((width // replicas, rows), f32),
        ),
        in_specs=[anywhere] * 9,
        out_specs=(anywhere, anywhere, anywhere),
        scratch_shapes=[block, block, block, block, pltpu.VMEM((1, width), f32)]
        + [pltpu.VMEM((rows, double), bf16)] * 2
        + [pltpu.VMEM((double, rows), bf16)] * 2
        + [pltpu.VMEM((replicas, width // replicas, rows), f32), by_seq, by_seq]
        + [by_group, by_device, by_group, by_device]
        + [pltpu.VMEM((steps * pairs, 8, rows), f32), pltpu.VMEM((steps, 8, rows), f32)]
        + [taps_spectrum, spectrum, spectrum, spectrum, taps_spectrum]
        + [by_device, by_group, by_device, by_group, by_seq, by_seq]
        + [pltpu.VMEM((width // 8, 8, rows), f32), dma((9,))]
        + [dma((n,)) for n in [steps] * 2 + [devices] * 8 + [steps] * 2 + [3]],
        compiler_params=pltpu.CompilerParams(
            collective_id=0, has_side_effects=True, vmem_limit_bytes=60 * 1024 * 1024
        ),
    )(
        inputs[0], gate_values[0], out_grad[0], filter_taps, skip_gain[None, :],
        *[jnp.asarray(table) for table in tables],
    )
    input_part, gate_part, filter_part = pl.pallas_call(
        hand_over,
        out_shape=tuple(jax.ShapeDtypeStruct(part.shape, part.dtype) for part in results),
        in_specs=[anywhere] * 3,
        out_specs=(anywhere,) * 3,
        scratch_shapes=[pltpu.VMEM(part.shape, part.dtype) for part in results] + [dma((6,))],
        compiler_params=pltpu.CompilerParams(vmem_limit_bytes=60 * 1024 * 1024),
    )(*results)
    return input_part[None], gate_part[None], filter_part.T


def solution(mesh):
    placed = (P("dp", "seq", None), P("dp", "seq", None), P("dp", "seq", None), P("seq", None), P())
    steps, replicas = mesh.shape["seq"], mesh.shape["dp"]

    def either(inputs, gate_values, out_grad, filter_taps, skip_gain):
        rows, width = filter_taps.shape
        fits = width == 4 * steps * replicas and replicas % 2 == 0 and rows % 128 == 0 and steps <= 8
        if fits and inputs.shape[0] == 1:
            return fused(inputs, gate_values, out_grad, filter_taps, skip_gain, steps, replicas)
        return local(inputs, gate_values, out_grad, filter_taps, skip_gain)

    return jax.shard_map(
        either,
        mesh=mesh,
        in_specs=placed,
        out_specs=(P("dp", "seq", None), P("dp", "seq", None), P("seq", "dp")),
        check_vma=False,
    )
```
